1024 devices in a mesh: rep: 8 (over x), node: 16 (over y, core), local: 8 (over z).
Axes of the slice: x: 8, y: 8, z: 8, core: 2. Of those that a mesh axis runs over, the one named last changes fastest.
Arguments:
- tokens: bfloat16 [16384, 2048], P(('rep', 'node', 'local')), may hold values from -6 to 6
- grads_out: bfloat16 [16384, 2048], P(('rep', 'node', 'local')), may hold values from -6 to 6
- expert_ids: int32 [16384, 8], P(('rep', 'node', 'local')), may hold values from 0 to 127, all different within a row; in each aligned block of 16 rows (0 to 15, 16 to 31, ...) at most 2 rows name the same one
- gates: bfloat16 [16384, 8], P(('rep', 'node', 'local')), may hold values from 0.019897461 to 0.29882812
- w_gate: bfloat16 [128, 2048, 384], P(('node', 'local')), may hold values from -0.125 to 0.125
- w_up: bfloat16 [128, 2048, 384], P(('node', 'local')), may hold values from -0.125 to 0.125
- w_down: bfloat16 [128, 384, 2048], P(('node', 'local')), may hold values from -0.3125 to 0.3125
Outputs:
- grad_tokens: bfloat16 [16384, 2048], P(('rep', 'node', 'local'))
- grad_gates: bfloat16 [16384, 8], P(('rep', 'node', 'local'))
- grad_w_gate: bfloat16 [128, 2048, 384], P(('node', 'local'), 'rep')
- grad_w_up: bfloat16 [128, 2048, 384], P(('node', 'local'), 'rep')
- grad_w_down: bfloat16 [128, 384, 2048], P(('node', 'local'), 'rep')
The draws below stay inside these ranges and needn't reach their ends.
Inputs may be any that keep to these rules, and one draw needn't show every extreme that they name: `expert_ids`: each row names 8 different experts. Among the 16 rows of one device no expert is named more than 2 times, and in some device's rows some expert is named exactly 2 times.
All inputs are finite; a program needn't handle non-finite values.
Results may differ from the reference program's by a relative error of at most 0.019.
Values may be sent and summed in bfloat16 or wider, within the bound.
No kernel may reach another device: no remote copies, remote signals or barrier semaphores. Data moves between devices by JAX's collectives and lax.ppermute only.
A program may use at most 64 MiB of HBM per device.

```python
import math
import jax
import jax.numpy as jnp
import numpy as np
from jax import lax

D = 2048
H = 384
TOP = 8
TOK_DEV = 16
E = 128
CAP = 2
TOKENS = 16384
N_REP = 8
N_NODE = 16
N_LOCAL = 8
DEVICES = 1024


def block_scale(rng, shape, pieces, least, high):
    def one(axis_at, shards_of):
        draws = jax.random.uniform(jax.random.fold_in(jax.random.fold_in(rng, 6), axis_at), (shards_of,), jnp.float32, least / len(pieces), high / len(pieces))
        return jnp.repeat(jnp.exp(draws), shape[axis_at] // shards_of).reshape((-1,) + (1,) * (len(shape) - axis_at - 1))

    factor_of = one(*pieces[0])
    for cut in pieces[1:]:
        factor_of = factor_of * one(*cut)
    return factor_of


def assign_block(stream_key, own, number, rows, amount, top, bound, slope):
    sequence = jax.random.permutation(stream_key, amount)
    crowded, common = shares(amount, rows * top, bound, slope, True), shares(amount, rows * top, bound, slope, False)
    places = jnp.arange(amount)

    def named(sizes, rotation):
        used = int((sizes > 0).sum())
        fixed = max(1, used // 4)
        moved = fixed + (places - fixed + rotation * (used - fixed)) % max(1, amount - fixed)
        return jnp.zeros((amount,), jnp.int32).at[sequence[jnp.where(places < fixed, places, moved)]].set(jnp.asarray(sizes, jnp.int32))

    sizes = jnp.where(number % 4 == 0, named(crowded, number // 4), named(common, number - number // 4 - 1))
    mixed = jax.random.permutation(jax.random.fold_in(own, 3), amount)
    giver, taker = mixed[0:amount // 2 * 2:2], mixed[1:amount // 2 * 2:2]
    room = jnp.minimum(sizes[giver] - 1, bound - sizes[taker]) // 2
    room = jnp.where((giver == sequence[0]) | (taker == sequence[0]) | (sizes[taker] == 0), 0, jnp.maximum(room, 0))
    moved = jax.random.randint(jax.random.fold_in(own, 4), (amount // 2,), 0, 1 << 20) % (room + 1)
    sizes = sizes.at[giver].add(-moved).at[taker].add(moved)
    members = jnp.searchsorted(jnp.cumsum(sizes), jnp.arange(rows * top), side="right").astype(jnp.int32)
    grid = members.reshape(top, rows).T
    grid = grid[jax.random.permutation(jax.random.fold_in(own, 1), rows)]
    rotation = jax.random.randint(jax.random.fold_in(own, 2), (rows, 1), 0, top)
    return jnp.take_along_axis(grid, (jnp.arange(top)[None, :] + rotation) % top, axis=1)


def shares(amount, total, bound, slope, full):
    weights = [(1 << 20) // math.isqrt(grade ** slope) + 1 for grade in range(1, amount + 1)]
    largest = bound if full else min(bound, max(-(-total // amount), total * weights[0] // sum(weights)))
    least = 1 if total - largest >= amount - 1 else 0
    given, rest = [largest] + [least] * (amount - 1), total - largest - least * (amount - 1)
    while rest > 0:
        free = [i for i in range(1, amount) if given[i] < largest] or [i for i in range(1, amount) if given[i] < bound]
        pool, remaining = sum([weights[i] for i in free]), rest
        for i in free:
            more = min(bound - given[i], max(1, remaining * weights[i] // pool), rest)
            given[i] = given[i] + more
            rest = rest - more
    return np.array(given)


def gaussian(rng, dims, spread, limit, cuts=(), held_as=jnp.bfloat16):
    drawn = spread * jax.random.normal(rng, dims, jnp.float32)
    if cuts:
        drawn = drawn * block_scale(rng, dims, cuts, -0.22, 0.18)
    return jnp.clip(drawn, -limit, limit).astype(held_as)


def setup_inputs(seed: int = 0) -> dict:
    streams_of = jax.random.split(jax.random.key(seed), 8)
    tokens = gaussian(streams_of[0], (TOKENS, D), 1.0, 6.0, ((0, 1024),))
    grads_out = gaussian(streams_of[1], (TOKENS, D), 1.0, 6.0, ((0, 1024),))
    expert_ids_keys = jax.random.split(jax.random.fold_in(streams_of[2], 1), TOKENS // TOK_DEV)
    expert_ids_turns = jax.random.permutation(jax.random.fold_in(streams_of[2], 3), TOKENS // TOK_DEV)
    expert_ids = jax.vmap(lambda own, number: assign_block(jax.random.fold_in(streams_of[2], 2), own, number, TOK_DEV, E, TOP, CAP, 2))(expert_ids_keys, expert_ids_turns).reshape((TOKENS, TOP))
    gates = jnp.clip(0.019897461 + 0.27893066 * jax.random.uniform(streams_of[3], (TOKENS, TOP), jnp.float32) ** block_scale(streams_of[3], (TOKENS, TOP), ((0, 1024),), -0.2, 0.2), 0.019897461, 0.29882812).astype(jnp.bfloat16)
    w_gate = gaussian(streams_of[4], (E, D, H), D ** -0.5, 0.125, ((0, 128),))
    w_up = gaussian(streams_of[5], (E, D, H), D ** -0.5, 0.125, ((0, 128),))
    w_down = gaussian(streams_of[6], (E, H, D), H ** -0.5, 0.3125, ((0, 128),))
    return {"tokens": tokens, "grads_out": grads_out, "expert_ids": expert_ids, "gates": gates, "w_gate": w_gate, "w_up": w_up, "w_down": w_down}


def expert_pass(routed_rows, incoming, weights, w_gate, w_up, w_down):
    gate_pre = jnp.dot(routed_rows, w_gate, preferred_element_type=jnp.float32)
    up_pre = jnp.dot(routed_rows, w_up, preferred_element_type=jnp.float32)
    sigmoid_gate = jax.nn.sigmoid(gate_pre)
    hidden_act = (gate_pre * sigmoid_gate * up_pre).astype(jnp.bfloat16)
    expert_out = jnp.dot(hidden_act, w_down, preferred_element_type=jnp.float32)
    gate_grads = jnp.sum(incoming.astype(jnp.float32) * expert_out, axis=-1).astype(jnp.bfloat16)
    cotangent = (weights.astype(jnp.float32)[:, None] * incoming.astype(jnp.float32)).astype(jnp.bfloat16)
    grad_act = lax.dot_general(cotangent, w_down, (((1,), (1,)), ((), ())), preferred_element_type=jnp.float32)
    grad_gate = (grad_act * up_pre * sigmoid_gate * (1.0 + gate_pre * (1.0 - sigmoid_gate))).astype(jnp.bfloat16)
    grad_up = (grad_act * gate_pre * sigmoid_gate).astype(jnp.bfloat16)
    grad_rows = lax.dot_general(grad_gate, w_gate, (((1,), (1,)), ((), ())), preferred_element_type=jnp.float32)
    grad_rows = grad_rows + lax.dot_general(grad_up, w_up, (((1,), (1,)), ((), ())), preferred_element_type=jnp.float32)
    return hidden_act, cotangent, grad_gate, grad_up, gate_grads, grad_rows.astype(jnp.bfloat16)


def slot_numbers(device_ids):
    flat_ids = device_ids.reshape(-1)
    onehot = (flat_ids[:, None] == jnp.arange(E, dtype=jnp.int32)[None, :]).astype(jnp.int32)
    before = jnp.cumsum(onehot, axis=0) - onehot
    return (flat_ids * CAP + jnp.sum(before * onehot, axis=1)).astype(jnp.int32)


def replica_sum(left_rows, right_rows):
    group_size = N_NODE * N_LOCAL
    left_full = left_rows.astype(jnp.float32).reshape(N_REP, group_size * CAP, left_rows.shape[1])
    right_full = right_rows.astype(jnp.float32).reshape(N_REP, group_size * CAP, right_rows.shape[1])
    partial_value = jnp.einsum('rnd,rnh->rdh', left_full, right_full).astype(jnp.bfloat16)
    return jnp.sum(partial_value.astype(jnp.float32), axis=0).astype(jnp.bfloat16)


def reference(tokens, grads_out, expert_ids, gates, w_gate, w_up, w_down):
    pair_count = TOK_DEV * TOP
    slot_ids = jax.vmap(slot_numbers)(expert_ids.reshape(DEVICES, TOK_DEV, TOP))
    device_rows = jnp.arange(DEVICES, dtype=jnp.int32)[:, None]
    slot_table = jnp.full((DEVICES, E * CAP), pair_count, jnp.int32)
    slot_table = slot_table.at[device_rows, slot_ids].set(jnp.arange(pair_count, dtype=jnp.int32)[None, :])
    slot_table = slot_table.reshape(DEVICES, E, CAP)
    flat_gates = gates.reshape(-1)

    def per_expert(totals, expert):
        grad_acc, weight_acc = totals
        chosen = lax.dynamic_index_in_dim(slot_table, expert, 1, keepdims=False)
        present_flat = (chosen < pair_count).reshape(-1)
        pair_global = (device_rows * pair_count + jnp.minimum(chosen, pair_count - 1)).reshape(-1).astype(jnp.int32)
        token_global = (pair_global // TOP).astype(jnp.int32)
        nothing = jnp.zeros((), jnp.bfloat16)
        routed_rows = jnp.where(present_flat[:, None], tokens[token_global], nothing)
        incoming = jnp.where(present_flat[:, None], grads_out[token_global], nothing)
        weights = jnp.where(present_flat, flat_gates[pair_global], nothing)
        hidden_act, cotangent, grad_gate, grad_up, gate_grads, grad_rows = expert_pass(
            routed_rows, incoming, weights, w_gate[expert], w_up[expert], w_down[expert])
        grad_acc = grad_acc.at[token_global].add(jnp.where(present_flat[:, None], grad_rows.astype(jnp.float32), jnp.zeros((), jnp.float32)))
        weight_acc = weight_acc.at[pair_global].add(jnp.where(present_flat, gate_grads.astype(jnp.float32), jnp.zeros((), jnp.float32)))
        sums = (replica_sum(routed_rows, grad_gate), replica_sum(routed_rows, grad_up), replica_sum(hidden_act, cotangent))
        return (grad_acc, weight_acc), sums

    initial = (jnp.zeros((TOKENS, D), jnp.float32), jnp.zeros((TOKENS * TOP,), jnp.float32))
    finals, stacked = lax.scan(per_expert, initial, jnp.arange(E, dtype=jnp.int32))
    grad_acc, weight_acc = finals
    sum_gate, sum_up, sum_down = stacked
    return (grad_acc.astype(jnp.bfloat16), weight_acc.reshape(TOKENS, TOP).astype(jnp.bfloat16),
            sum_gate, sum_up, sum_down)
```

```python
import jax
import jax.numpy as jnp
from jax import lax
from jax.sharding import PartitionSpec as P

PLANE = ("node", "local")


def exchange(blocks):
    return lax.all_to_all(blocks, PLANE, split_axis=0, concat_axis=0, tiled=True)


def dot(left, right, left_dim, right_dim):
    return lax.dot_general(
        left, right, (((left_dim,), (right_dim,)), ((), ())), preferred_element_type=jnp.float32
    )


def shards(tokens, grads_out, expert_ids, gates, w_gate, w_up, w_down):
    experts = lax.axis_size("node") * lax.axis_size("local")
    tok_dev, top_count = expert_ids.shape
    model_width = tokens.shape[1]
    hidden = w_gate.shape[2]
    pairs = tok_dev * top_count
    capacity = max(1, 2 * pairs // experts)
    slot_count = experts * capacity
    w_gate, w_up, w_down = w_gate[0], w_up[0], w_down[0]

    flat_ids = expert_ids.reshape(-1)
    earlier = lax.iota(jnp.int32, pairs)[:, None] > lax.iota(jnp.int32, pairs)[None, :]
    same = flat_ids[:, None] == flat_ids[None, :]
    rank = jnp.sum((same & earlier).astype(jnp.int32), axis=1)
    slot_index = flat_ids * capacity + rank
    placed = lax.iota(jnp.int32, slot_count)[:, None] == slot_index[None, :]
    placed = placed.astype(jnp.bfloat16)
    owners = lax.iota(jnp.int32, pairs) // top_count
    owned = owners[:, None] == lax.iota(jnp.int32, tok_dev)[None, :]
    flat_gates = gates.reshape(-1)
    zero = jnp.zeros((), jnp.bfloat16)
    spread = dot(placed, owned.astype(jnp.bfloat16), 1, 0).astype(jnp.bfloat16)
    weighted = dot(placed, jnp.where(owned, flat_gates[:, None], zero), 1, 0).astype(jnp.bfloat16)

    def send(spreader, rows):
        blocks = dot(spreader, rows, 1, 0).astype(jnp.bfloat16)
        blocks = blocks.reshape(experts, capacity, model_width)
        return exchange(blocks).reshape(slot_count, model_width)

    routed = send(spread, tokens)
    cotangent = send(weighted, grads_out)

    gate_pre = dot(routed, w_gate, 1, 0)
    up_pre = dot(routed, w_up, 1, 0)
    sigmoid_gate = jax.nn.sigmoid(gate_pre)
    silu_gate = gate_pre * sigmoid_gate
    hidden_act = (silu_gate * up_pre).astype(jnp.bfloat16)
    slope = up_pre * sigmoid_gate * (1.0 + gate_pre * (1.0 - sigmoid_gate))

    grad_act = dot(cotangent, w_down, 1, 1)
    grad_gate = (grad_act * slope).astype(jnp.bfloat16)
    grad_up = (grad_act * silu_gate).astype(jnp.bfloat16)

    def reduce(partial):
        return lax.psum_scatter(
            partial.astype(jnp.bfloat16), "rep", scatter_dimension=0, tiled=True
        )

    gate_up = jnp.concatenate((grad_gate, grad_up), axis=1)
    gate_up_sum = reduce(dot(routed, gate_up, 0, 0))
    down_sum = reduce(dot(hidden_act, cotangent, 0, 0))

    gate_score = jnp.sum(hidden_act.astype(jnp.float32) * grad_act, axis=1).astype(jnp.bfloat16)
    grad_rows = (dot(grad_gate, w_gate, 1, 1) + dot(grad_up, w_up, 1, 1)).astype(jnp.bfloat16)
    returned_score = exchange(gate_score.reshape(experts, capacity)).reshape(slot_count)
    returned = exchange(grad_rows.reshape(experts, capacity, model_width))
    returned = returned.reshape(slot_count, model_width)

    grad_tokens = dot(spread, returned, 0, 0).astype(jnp.bfloat16)
    score = dot(returned_score[None, :], placed, 1, 0).reshape(tok_dev, top_count)
    grad_gates = (score / gates.astype(jnp.float32)).astype(jnp.bfloat16)
    return (
        grad_tokens,
        grad_gates,
        gate_up_sum[None, :, :hidden],
        gate_up_sum[None, :, hidden:],
        down_sum[None],
    )


def solution(mesh):
    rows = P(("rep", "node", "local"), None)
    weights = P(PLANE, None, None)
    sharded = P(PLANE, "rep", None)
    return jax.shard_map(
        shards,
        mesh=mesh,
        in_specs=(rows, rows, rows, rows, weights, weights, weights),
        out_specs=(rows, rows, sharded, sharded, sharded),
        check_vma=False,
    )
```

```python
import jax
import jax.numpy as jnp
from jax import lax
from jax.experimental import pallas as pl
from jax.experimental.pallas import tpu as pltpu
from jax.sharding import PartitionSpec as P

PLANE = ("node", "local")
BF16, F32, I32 = jnp.bfloat16, jnp.float32, jnp.int32
VMEM_LIMIT = 48 << 20
CAP, PIECES, WIDE = 2, 8, 256
BLOCK = CAP * PIECES
GROUP = 16
GROUP_SLOTS = GROUP * CAP
LANES = 128


def iota(shape, dim):
    return lax.broadcasted_iota(I32, shape, dim)


def dot(left, right, left_dim, right_dim):
    return lax.dot_general(
        left, right, (((left_dim,), (right_dim,)), ((), ())), preferred_element_type=F32
    )


def whole(count):
    return [pl.BlockSpec(memory_space=pltpu.VMEM)] * count


def call(body, outs, in_specs, out_specs, scratch=(), cost=None):
    return pl.pallas_call(
        body,
        out_shape=outs,
        in_specs=in_specs,
        out_specs=out_specs,
        scratch_shapes=scratch,
        cost_estimate=cost,
        compiler_params=pltpu.CompilerParams(vmem_limit_bytes=VMEM_LIMIT),
    )


def route_body(ids_ref, gates_ref, tokens_ref, grads_ref, out_ref, spread_ref):
    top, tok = ids_ref.shape
    slots = spread_ref.shape[0]
    ids = jnp.concatenate([ids_ref[...]] * (LANES // tok), axis=1)
    weights = jnp.concatenate([gates_ref[...].astype(F32)] * (LANES // tok), axis=1)
    expert = iota((slots, LANES), 0) // CAP
    named = jnp.zeros((slots, LANES), F32)
    weight = jnp.zeros((slots, LANES), F32)
    for k in range(top):
        hit = expert == ids[k : k + 1]
        named = named + jnp.where(hit, 1.0, 0.0)
        weight = weight + jnp.where(hit, weights[k : k + 1], 0.0)
    before, after = iota((LANES, LANES), 0), iota((LANES, LANES), 1)
    earlier = (before // tok == after // tok) & (before < after)
    rank = dot(named.astype(BF16), jnp.where(earlier, 1.0, 0.0).astype(BF16), 1, 0)
    mine = rank == (iota((slots, LANES), 0) % CAP).astype(F32)
    spread = jnp.where(mine, named, 0.0).astype(BF16)
    weighted = jnp.where(mine, weight, 0.0).astype(BF16)
    spread_ref[...] = spread
    rows = GROUP * BLOCK
    row = iota((rows, GROUP_SLOTS), 0)
    expand = (row // BLOCK) * CAP + row % CAP == iota((rows, GROUP_SLOTS), 1)
    expand = jnp.where(expand, 1.0, 0.0).astype(BF16)
    piece = (iota((rows, LANES), 0) % BLOCK) // CAP == iota((rows, LANES), 1) // tok
    for part, (chosen, ref) in enumerate(((spread, tokens_ref), (weighted, grads_ref))):
        pieces = [ref[:, j * WIDE : (j + 1) * WIDE] for j in range(PIECES)]
        source = jnp.concatenate(pieces, axis=0)
        for g in range(slots // GROUP_SLOTS):
            picked = chosen[g * GROUP_SLOTS : (g + 1) * GROUP_SLOTS]
            select = jnp.where(piece, dot(expand, picked, 1, 0), 0.0).astype(BF16)
            block = dot(select, source, 1, 0).astype(BF16)
            out_ref[g * GROUP : (g + 1) * GROUP, part * BLOCK : (part + 1) * BLOCK, :] = (
                block.reshape(GROUP, BLOCK, WIDE)
            )


def expert_body(
    arrived_ref, gate_hbm, up_hbm, down_hbm,
    partial_hbm, slopes_ref, score_ref,
    rows_ref, w_gate, w_up, w_down, packed, load_sems, store_sems,
):
    loads = [
        pltpu.make_async_copy(source, target, load_sems.at[i])
        for i, (source, target) in enumerate(
            ((gate_hbm, w_gate), (up_hbm, w_up), (down_hbm, w_down))
        )
    ]
    for load in loads:
        load.start()
    slots = rows_ref.shape[1]
    hidden = w_gate.shape[1]
    order = iota((GROUP * BLOCK, GROUP * BLOCK), 0)
    wanted = (order // CAP % GROUP) * BLOCK + (order // GROUP_SLOTS) * CAP + order % CAP
    shuffle = jnp.where(wanted == iota(order.shape, 1), 1.0, 0.0).astype(BF16)
    for part in range(2):
        for g in range(slots // GROUP_SLOTS):
            block = arrived_ref[g * GROUP : (g + 1) * GROUP, part * BLOCK : (part + 1) * BLOCK, :]
            block = dot(shuffle, block.reshape(GROUP * BLOCK, WIDE), 1, 0).astype(BF16)
            for j in range(PIECES):
                rows_ref[
                    part, g * GROUP_SLOTS : (g + 1) * GROUP_SLOTS, j * WIDE : (j + 1) * WIDE
                ] = block[j * GROUP_SLOTS : (j + 1) * GROUP_SLOTS]
    loads[0].wait()
    gate_pre = dot(rows_ref[0], w_gate[...], 1, 0)
    loads[1].wait()
    up_pre = dot(rows_ref[0], w_up[...], 1, 0)
    loads[2].wait()
    grad_act = dot(rows_ref[1], w_down[...], 1, 1)
    sigmoid_gate = 1.0 / (1.0 + jnp.exp(-gate_pre))
    silu_gate = gate_pre * sigmoid_gate
    hidden_act = (silu_gate * up_pre).astype(BF16)
    slope = up_pre * sigmoid_gate * (1.0 + gate_pre * (1.0 - sigmoid_gate))
    slopes_ref[:, :hidden] = (grad_act * slope).astype(BF16)
    slopes_ref[:, hidden:] = (grad_act * silu_gate).astype(BF16)
    score = jnp.sum(hidden_act.astype(F32) * grad_act, axis=1, keepdims=True)
    score_ref[...] = jnp.broadcast_to(score, score_ref.shape).astype(BF16)

    shards = packed.shape[0]
    share = hidden // shards
    gate_up_rows = 2 * hidden // LANES * WIDE
    for n in range(PIECES):
        down = dot(hidden_act, rows_ref[1, :, n * WIDE : (n + 1) * WIDE], 0, 0).astype(BF16)
        for s in range(shards):
            for b in range(WIDE // LANES):
                at = gate_up_rows + (n * (WIDE // LANES) + b) * share
                packed[s, at : at + share, :] = down[
                    s * share : (s + 1) * share, b * LANES : (b + 1) * LANES
                ]
    stores = []
    for s in range(shards):
        columns = slice(s * WIDE, (s + 1) * WIDE)
        gate_up = dot(rows_ref[0, :, columns], slopes_ref[...], 0, 0).astype(BF16)
        for b in range(2 * hidden // LANES):
            packed[s, b * WIDE : (b + 1) * WIDE, :] = gate_up[:, b * LANES : (b + 1) * LANES]
        store = pltpu.make_async_copy(packed.at[s], partial_hbm.at[s], store_sems.at[s])
        store.start()
        stores.append(store)
    for store in stores:
        store.wait()


def rows_body(slopes_ref, score_ref, gate_ref, up_ref, out_ref):
    hidden = gate_ref.shape[1]
    width = gate_ref.shape[0]
    for j in range(width // WIDE):
        columns = slice(j * WIDE, (j + 1) * WIDE)
        rows = dot(slopes_ref[:, :hidden], gate_ref[columns, :], 1, 1)
        rows = rows + dot(slopes_ref[:, hidden:], up_ref[columns, :], 1, 1)
        out_ref[:, columns] = rows.astype(BF16)
    out_ref[:, width:] = score_ref[...]


def combine_body(returned_ref, spread_ref, ids_ref, gates_ref, tokens_ref, out_gates_ref):
    top, tok = ids_ref.shape
    width = tokens_ref.shape[1]
    slots = spread_ref.shape[0]
    spread = spread_ref[:, :tok]
    for j in range(width // WIDE):
        columns = slice(j * WIDE, (j + 1) * WIDE)
        tokens_ref[:, columns] = dot(spread, returned_ref[:, columns], 0, 0).astype(BF16)
    score = returned_ref[:, width : width + tok].astype(F32) * spread.astype(F32)
    expert = iota((slots, tok), 0) // CAP
    gates = gates_ref[...].astype(F32)
    sums = [
        jnp.sum(jnp.where(expert == ids_ref[k : k + 1, :], score, 0.0), axis=0, keepdims=True)
        for k in range(top)
    ]
    out_gates_ref[...] = (jnp.concatenate(sums, axis=0) / gates).astype(BF16)


def unpack_body(sums_ref, gate_ref, up_ref, down_ref):
    hidden = gate_ref.shape[1]
    share = down_ref.shape[0]
    blocks = hidden // LANES
    for b in range(blocks):
        columns = slice(b * LANES, (b + 1) * LANES)
        gate_ref[:, columns] = sums_ref[b * WIDE : (b + 1) * WIDE, :]
        up_ref[:, columns] = sums_ref[(blocks + b) * WIDE : (blocks + b + 1) * WIDE, :]
    for b in range(down_ref.shape[1] // LANES):
        at = 2 * blocks * WIDE + b * share
        down_ref[:, b * LANES : (b + 1) * LANES] = sums_ref[at : at + share, :]


def shaped(*shape, dtype=BF16):
    return jax.ShapeDtypeStruct(shape, dtype)


def cost(flops, bytes_accessed):
    return pl.CostEstimate(flops=flops, bytes_accessed=bytes_accessed, transcendentals=0)


def exchange(blocks):
    return lax.all_to_all(blocks, PLANE, split_axis=0, concat_axis=0, tiled=True)


def shards(tokens, grads_out, expert_ids, gates, w_gate, w_up, w_down):
    experts = lax.axis_size("node") * lax.axis_size("local")
    reps = lax.axis_size("rep")
    tok, top = expert_ids.shape
    width = tokens.shape[1]
    hidden = w_gate.shape[2]
    slots = experts * CAP
    w_gate, w_up, w_down = w_gate[0], w_up[0], w_down[0]
    ids_t, gates_t = expert_ids.T, gates.T
    packed_rows = (2 * hidden * (width // reps) + (hidden // reps) * width) // LANES
    product = 2 * slots * width * hidden

    outgoing, spread = call(
        route_body,
        (shaped(experts, 2 * BLOCK, WIDE), shaped(slots, LANES)),
        whole(4),
        whole(2),
        cost=cost(4 * slots * LANES * width, 4 * slots * width),
    )(ids_t, gates_t, tokens, grads_out)
    arrived = exchange(outgoing)

    hbm = pl.BlockSpec(memory_space=pl.ANY)
    partial, slopes, score = call(
        expert_body,
        (
            shaped(reps, packed_rows, LANES),
            shaped(slots, 2 * hidden),
            shaped(slots, LANES),
        ),
        whole(1) + [hbm] * 3,
        [hbm] + whole(2),
        scratch=(
            pltpu.VMEM((2, slots, width), BF16),
            pltpu.VMEM((width, hidden), BF16),
            pltpu.VMEM((width, hidden), BF16),
            pltpu.VMEM((hidden, width), BF16),
            pltpu.VMEM((reps, packed_rows, LANES), BF16),
            pltpu.SemaphoreType.DMA((3,)),
            pltpu.SemaphoreType.DMA((reps,)),
        ),
        cost=cost(6 * product, 12 << 20),
    )(arrived, w_gate, w_up, w_down)

    sums = lax.psum_scatter(
        partial.reshape(reps * packed_rows, LANES), "rep", scatter_dimension=0, tiled=True
    )

    rows = call(
        rows_body,
        shaped(slots, width + LANES),
        whole(4),
        whole(1)[0],
        cost=cost(2 * product, 5 << 20),
    )(slopes, score, w_gate, w_up)
    returned = exchange(rows.reshape(experts, CAP, width + LANES)).reshape(slots, width + LANES)
    grad_tokens, grad_gates = call(
        combine_body,
        (shaped(tok, width), shaped(top, tok)),
        whole(4),
        whole(2),
        cost=cost(2 * slots * tok * width, 2 << 20),
    )(returned, spread, ids_t, gates_t)

    grad_w_gate, grad_w_up, grad_w_down = call(
        unpack_body,
        (
            shaped(width // reps, hidden),
            shaped(width // reps, hidden),
            shaped(hidden // reps, width),
        ),
        whole(1),
        whole(3),
        cost=cost(0, 2 << 20),
    )(sums)
    return (
        grad_tokens,
        grad_gates.T,
        grad_w_gate[None],
        grad_w_up[None],
        grad_w_down[None],
    )


def solution(mesh):
    rows = P(("rep", "node", "local"), None)
    weights = P(PLANE, None, None)
    sharded = P(PLANE, "rep", None)
    return jax.shard_map(
        shards,
        mesh=mesh,
        in_specs=(rows, rows, rows, rows, weights, weights, weights),
        out_specs=(rows, rows, sharded, sharded, sharded),
        check_vma=False,
    )
```

```python
import jax
import jax.numpy as jnp
from jax import lax
from jax.experimental import pallas as pl
from jax.experimental.pallas import tpu as pltpu
from jax.sharding import PartitionSpec as P

PLANE = ("node", "local")
BF16, F32, I32 = jnp.bfloat16, jnp.float32, jnp.int32
VMEM_LIMIT = 48 << 20
CAP, PIECES, WIDE = 2, 8, 256
BLOCK = CAP * PIECES
GROUP = 16
GROUP_SLOTS = GROUP * CAP
LANES = 128


def iota(shape, dim):
    return lax.broadcasted_iota(I32, shape, dim)


def dot(left, right, left_dim, right_dim):
    return lax.dot_general(
        left, right, (((left_dim,), (right_dim,)), ((), ())), preferred_element_type=F32
    )


def whole(count):
    return [pl.BlockSpec(memory_space=pltpu.VMEM)] * count


def call(body, outs, in_specs, out_specs, scratch=(), cost=None):
    return pl.pallas_call(
        body,
        out_shape=outs,
        in_specs=in_specs,
        out_specs=out_specs,
        scratch_shapes=scratch,
        cost_estimate=cost,
        compiler_params=pltpu.CompilerParams(vmem_limit_bytes=VMEM_LIMIT),
    )


def route_body(
    ids_hbm, gates_ref, tokens_hbm, grads_hbm, out_ref, spread_ref,
    ids_ref, tokens_ref, grads_ref, sems,
):
    loads = [
        pltpu.make_async_copy(source, target, sems.at[i])
        for i, (source, target) in enumerate(
            ((ids_hbm, ids_ref), (tokens_hbm, tokens_ref), (grads_hbm, grads_ref))
        )
    ]
    for load in loads:
        load.start()
    top, tok = ids_ref.shape
    loads[0].wait()
    slots = spread_ref.shape[0]
    ids = jnp.concatenate([ids_ref[...]] * (LANES // tok), axis=1)
    weights = jnp.concatenate([gates_ref[...].astype(F32)] * (LANES // tok), axis=1)
    expert = iota((slots, LANES), 0) // CAP
    named = jnp.zeros((slots, LANES), F32)
    weight = jnp.zeros((slots, LANES), F32)
    for k in range(top):
        hit = expert == ids[k : k + 1]
        named = named + jnp.where(hit, 1.0, 0.0)
        weight = weight + jnp.where(hit, weights[k : k + 1], 0.0)
    before, after = iota((LANES, LANES), 0), iota((LANES, LANES), 1)
    earlier = (before // tok == after // tok) & (before < after)
    rank = dot(named.astype(BF16), jnp.where(earlier, 1.0, 0.0).astype(BF16), 1, 0)
    mine = rank == (iota((slots, LANES), 0) % CAP).astype(F32)
    spread = jnp.where(mine, named, 0.0).astype(BF16)
    weighted = jnp.where(mine, weight, 0.0).astype(BF16)
    spread_ref[...] = spread
    rows = GROUP * BLOCK
    row = iota((rows, GROUP_SLOTS), 0)
    expand = (row // BLOCK) * CAP + row % CAP == iota((rows, GROUP_SLOTS), 1)
    expand = jnp.where(expand, 1.0, 0.0).astype(BF16)
    piece = (iota((rows, LANES), 0) % BLOCK) // CAP == iota((rows, LANES), 1) // tok
    for part, (chosen, ref) in enumerate(((spread, tokens_ref), (weighted, grads_ref))):
        loads[part + 1].wait()
        pieces = [ref[:, j * WIDE : (j + 1) * WIDE] for j in range(PIECES)]
        source = jnp.concatenate(pieces, axis=0)
        for g in range(slots // GROUP_SLOTS):
            picked = chosen[g * GROUP_SLOTS : (g + 1) * GROUP_SLOTS]
            select = jnp.where(piece, dot(expand, picked, 1, 0), 0.0).astype(BF16)
            block = dot(select, source, 1, 0).astype(BF16)
            out_ref[g * GROUP : (g + 1) * GROUP, part * BLOCK : (part + 1) * BLOCK, :] = (
                block.reshape(GROUP, BLOCK, WIDE)
            )


def expert_body(
    order_ref, arrived_ref, gate_hbm, up_hbm, down_hbm,
    slopes_ref, score_ref, far_ahead, far_behind, *refs,
):
    near, (rows_ref, w_gate, w_up, w_down, down_ref, load_sems) = refs[:-6], refs[-6:]
    loads = [
        pltpu.make_async_copy(source, target, load_sems.at[i])
        for i, (source, target) in enumerate(
            ((gate_hbm, w_gate), (up_hbm, w_up), (down_hbm, w_down))
        )
    ]
    for load in loads:
        load.start()
    slots = rows_ref.shape[1]
    hidden = w_gate.shape[1]
    order = iota((GROUP * BLOCK, GROUP * BLOCK), 0)
    wanted = (order // CAP % GROUP) * BLOCK + (order // GROUP_SLOTS) * CAP + order % CAP
    shuffle = jnp.where(wanted == iota(order.shape, 1), 1.0, 0.0).astype(BF16)
    for part in range(2):
        for g in range(slots // GROUP_SLOTS):
            block = arrived_ref[g * GROUP : (g + 1) * GROUP, part * BLOCK : (part + 1) * BLOCK, :]
            block = dot(shuffle, block.reshape(GROUP * BLOCK, WIDE), 1, 0).astype(BF16)
            for j in range(PIECES):
                rows_ref[
                    part, g * GROUP_SLOTS : (g + 1) * GROUP_SLOTS, j * WIDE : (j + 1) * WIDE
                ] = block[j * GROUP_SLOTS : (j + 1) * GROUP_SLOTS]
    loads[0].wait()
    gate_pre = dot(rows_ref[0], w_gate[...], 1, 0)
    loads[1].wait()
    up_pre = dot(rows_ref[0], w_up[...], 1, 0)
    loads[2].wait()
    grad_act = dot(rows_ref[1], w_down[...], 1, 1)
    sigmoid_gate = 1.0 / (1.0 + jnp.exp(-gate_pre))
    silu_gate = gate_pre * sigmoid_gate
    hidden_act = (silu_gate * up_pre).astype(BF16)
    slope = up_pre * sigmoid_gate * (1.0 + gate_pre * (1.0 - sigmoid_gate))
    slopes_ref[:, :hidden] = (grad_act * slope).astype(BF16)
    slopes_ref[:, hidden:] = (grad_act * silu_gate).astype(BF16)
    score = jnp.sum(hidden_act.astype(F32) * grad_act, axis=1, keepdims=True)
    score_ref[...] = jnp.broadcast_to(score, score_ref.shape).astype(BF16)

    shards = order_ref.shape[0]
    share = hidden // shards
    for n in range(PIECES):
        columns = slice(n * WIDE, (n + 1) * WIDE)
        down_ref[:, columns] = dot(hidden_act, rows_ref[1, :, columns], 0, 0).astype(BF16)
    far = shards // 2
    for offset in (far, *range(far), *range(far + 1, shards)):
        target = order_ref[offset]
        columns = pl.ds(pl.multiple_of(target * WIDE, WIDE), WIDE)
        gate_up = dot(rows_ref[0, :, columns], slopes_ref[...], 0, 0).astype(BF16)
        down = down_ref[pl.ds(pl.multiple_of(target * share, 16), share), :]
        pieces = [gate_up[:, b * LANES : (b + 1) * LANES] for b in range(2 * hidden // LANES)]
        pieces += [down[:, b * LANES : (b + 1) * LANES] for b in range(down.shape[1] // LANES)]
        at = 0
        for piece in pieces:
            rows = piece.shape[0]
            if offset != far:
                near[offset - (offset > far)][at : at + rows, :] = piece
            else:
                split = far_ahead.shape[0]
                first = min(max(split - at, 0), rows)
                if first:
                    far_ahead[at : at + first, :] = piece[:first]
                if first < rows:
                    far_behind[at + first - split : at + rows - split, :] = piece[first:]
            at += rows


def rows_body(slopes_ref, score_ref, gate_ref, up_ref, out_ref):
    hidden = gate_ref.shape[1]
    width = gate_ref.shape[0]
    for j in range(width // WIDE):
        columns = slice(j * WIDE, (j + 1) * WIDE)
        rows = dot(slopes_ref[:, :hidden], gate_ref[columns, :], 1, 1)
        rows = rows + dot(slopes_ref[:, hidden:], up_ref[columns, :], 1, 1)
        out_ref[:, columns] = rows.astype(BF16)
    out_ref[:, width:] = score_ref[...]


def combine_body(returned_ref, spread_ref, ids_ref, gates_ref, tokens_ref, out_gates_ref):
    top, tok = ids_ref.shape
    width = tokens_ref.shape[1]
    slots = spread_ref.shape[0]
    spread = spread_ref[:, :tok]
    for j in range(width // WIDE):
        columns = slice(j * WIDE, (j + 1) * WIDE)
        tokens_ref[:, columns] = dot(spread, returned_ref[:, columns], 0, 0).astype(BF16)
    score = returned_ref[:, width : width + tok].astype(F32) * spread.astype(F32)
    expert = iota((slots, tok), 0) // CAP
    gates = gates_ref[...].astype(F32)
    sums = [
        jnp.sum(jnp.where(expert == ids_ref[k : k + 1, :], score, 0.0), axis=0, keepdims=True)
        for k in range(top)
    ]
    out_gates_ref[...] = (jnp.concatenate(sums, axis=0) / gates).astype(BF16)


def unpack_body(own_ref, ahead_ref, behind_ref, gate_ref, up_ref, down_ref):
    hidden = gate_ref.shape[1]
    share = down_ref.shape[0]
    blocks = hidden // LANES

    def total(at, rows):
        at = slice(at, at + rows)
        parts = [ref[at, :].astype(F32) for ref in (own_ref, ahead_ref, behind_ref)]
        return (parts[0] + parts[1] + parts[2]).astype(BF16)

    for b in range(blocks):
        columns = slice(b * LANES, (b + 1) * LANES)
        gate_ref[:, columns] = total(b * WIDE, WIDE)
        up_ref[:, columns] = total((blocks + b) * WIDE, WIDE)
    for b in range(down_ref.shape[1] // LANES):
        at = 2 * blocks * WIDE + b * share
        down_ref[:, b * LANES : (b + 1) * LANES] = total(at, share)


def shaped(*shape, dtype=BF16):
    return jax.ShapeDtypeStruct(shape, dtype)


def cost(flops, bytes_accessed):
    return pl.CostEstimate(flops=flops, bytes_accessed=bytes_accessed, transcendentals=0)


def exchange(blocks):
    return lax.all_to_all(blocks, PLANE, split_axis=0, concat_axis=0, tiled=True)


def ring(phase):
    reps, nodes = lax.axis_size("rep"), lax.axis_size("node")
    pairs = []
    for r in range(reps):
        for n in range(nodes):
            step = 1 if n % 2 == phase else -1
            pairs.append((r * nodes + n, (r + step) % reps * nodes + n))
    return lambda message: lax.ppermute(message, ("rep", "node"), pairs)


def add(left, right):
    return (left.astype(F32) + right.astype(F32)).astype(BF16)


def reduce_scatter(far_ahead, far_behind, near):
    forward, backward = ring(0), ring(1)
    half = far_ahead.shape[0]
    ahead, behind = forward(far_ahead), backward(far_behind)
    last = len(near) // 2
    for d in range(last, 0, -1):
        to_ahead, to_behind = near[d], near[len(near) - d]
        if d == last:
            to_ahead = jnp.concatenate((add(to_ahead[:half], ahead), to_ahead[half:]))
            to_behind = jnp.concatenate((to_behind[:half], add(to_behind[half:], behind)))
        else:
            to_ahead, to_behind = add(to_ahead, ahead), add(to_behind, behind)
        ahead, behind = forward(to_ahead), backward(to_behind)
    return near[0], ahead, behind


def shards(tokens, grads_out, expert_ids, gates, w_gate, w_up, w_down):
    experts = lax.axis_size("node") * lax.axis_size("local")
    reps = lax.axis_size("rep")
    tok, top = expert_ids.shape
    width = tokens.shape[1]
    hidden = w_gate.shape[2]
    slots = experts * CAP
    w_gate, w_up, w_down = w_gate[0], w_up[0], w_down[0]
    ids_t, gates_t = expert_ids.T, gates.T
    packed_rows = (2 * hidden * (width // reps) + (hidden // reps) * width) // LANES
    product = 2 * slots * width * hidden

    hbm = pl.BlockSpec(memory_space=pl.ANY)
    outgoing, spread = call(
        route_body,
        (shaped(experts, 2 * BLOCK, WIDE), shaped(slots, LANES)),
        [hbm] + whole(1) + [hbm] * 2,
        whole(2),
        scratch=(
            pltpu.VMEM((top, tok), I32),
            pltpu.VMEM((tok, width), BF16),
            pltpu.VMEM((tok, width), BF16),
            pltpu.SemaphoreType.DMA((3,)),
        ),
        cost=cost(4 * slots * LANES * width, 4 * slots * width),
    )(ids_t, gates_t, tokens, grads_out)
    arrived = exchange(outgoing)

    direction = 1 - 2 * (lax.axis_index("node") % 2)
    order = (lax.axis_index("rep") + direction * lax.iota(I32, reps) + reps) % reps
    slopes, score, far_ahead, far_behind, *near = call(
        expert_body,
        (
            shaped(slots, 2 * hidden),
            shaped(slots, LANES),
            *[shaped(packed_rows // 2, LANES)] * 2,
            *[shaped(packed_rows, LANES)] * (reps - 1),
        ),
        [pl.BlockSpec(memory_space=pltpu.SMEM)] + whole(1) + [hbm] * 3,
        whole(4 + reps - 1),
        scratch=(
            pltpu.VMEM((2, slots, width), BF16),
            pltpu.VMEM((width, hidden), BF16),
            pltpu.VMEM((width, hidden), BF16),
            pltpu.VMEM((hidden, width), BF16),
            pltpu.VMEM((hidden, width), BF16),
            pltpu.SemaphoreType.DMA((3,)),
        ),
        cost=cost(6 * product, 12 << 20),
    )(order, arrived, w_gate, w_up, w_down)

    sums = reduce_scatter(far_ahead, far_behind, near)

    rows = call(
        rows_body,
        shaped(slots, width + LANES),
        whole(4),
        whole(1)[0],
        cost=cost(2 * product, 5 << 20),
    )(slopes, score, w_gate, w_up)
    returned = exchange(rows.reshape(experts, CAP, width + LANES)).reshape(slots, width + LANES)
    grad_tokens, grad_gates = call(
        combine_body,
        (shaped(tok, width), shaped(top, tok)),
        whole(4),
        whole(2),
        cost=cost(2 * slots * tok * width, 2 << 20),
    )(returned, spread, ids_t, gates_t)

    grad_w_gate, grad_w_up, grad_w_down = call(
        unpack_body,
        (
            shaped(width // reps, hidden),
            shaped(width // reps, hidden),
            shaped(hidden // reps, width),
        ),
        whole(3),
        whole(3),
        cost=cost(0, 2 << 20),
    )(*sums)
    return (
        grad_tokens,
        grad_gates.T,
        grad_w_gate[None],
        grad_w_up[None],
        grad_w_down[None],
    )


def solution(mesh):
    rows = P(("rep", "node", "local"), None)
    weights = P(PLANE, None, None)
    sharded = P(PLANE, "rep", None)
    return jax.shard_map(
        shards,
        mesh=mesh,
        in_specs=(rows, rows, rows, rows, weights, weights, weights),
        out_specs=(rows, rows, sharded, sharded, sharded),
        check_vma=False,
    )
```

```python
import jax
import jax.numpy as jnp
from jax import lax
from jax.experimental import pallas as pl
from jax.experimental.pallas import tpu as pltpu
from jax.sharding import PartitionSpec as P

PLANE = ("node", "local")
BF16, F32, I32 = jnp.bfloat16, jnp.float32, jnp.int32
VMEM_LIMIT, VMEM_MOST = 24 << 20, 60 << 20
CAP, PIECES, WIDE = 2, 8, 256
BLOCK = CAP * PIECES
GROUP = 16
GROUP_SLOTS = GROUP * CAP
LANES = 128


def iota(shape, dim):
    return lax.broadcasted_iota(I32, shape, dim)


def dot(left, right, left_dim, right_dim):
    return lax.dot_general(
        left, right, (((left_dim,), (right_dim,)), ((), ())), preferred_element_type=F32
    )


def whole(count):
    return [pl.BlockSpec(memory_space=pltpu.VMEM)] * count


def call(body, outs, in_specs, out_specs, scratch=(), cost=None, limit=VMEM_LIMIT):
    return pl.pallas_call(
        body,
        out_shape=outs,
        in_specs=in_specs,
        out_specs=out_specs,
        scratch_shapes=scratch,
        cost_estimate=cost,
        compiler_params=pltpu.CompilerParams(vmem_limit_bytes=limit),
    )


def route_body(
    ids_hbm, gates_ref, tokens_hbm, grads_hbm, out_ref, spread_ref,
    ids_ref, tokens_ref, grads_ref, sems,
):
    loads = [
        pltpu.make_async_copy(source, target, sems.at[i])
        for i, (source, target) in enumerate(
            ((ids_hbm, ids_ref), (tokens_hbm, tokens_ref), (grads_hbm, grads_ref))
        )
    ]
    for load in loads:
        load.start()
    top, tok = ids_ref.shape
    loads[0].wait()
    slots = spread_ref.shape[0]
    ids = jnp.concatenate([ids_ref[...]] * (LANES // tok), axis=1)
    weights = jnp.concatenate([gates_ref[...].astype(F32)] * (LANES // tok), axis=1)
    expert = iota((slots, LANES), 0) // CAP
    named = jnp.zeros((slots, LANES), F32)
    weight = jnp.zeros((slots, LANES), F32)
    for k in range(top):
        hit = expert == ids[k : k + 1]
        named = named + jnp.where(hit, 1.0, 0.0)
        weight = weight + jnp.where(hit, weights[k : k + 1], 0.0)
    before, after = iota((LANES, LANES), 0), iota((LANES, LANES), 1)
    earlier = (before // tok == after // tok) & (before < after)
    rank = dot(named.astype(BF16), jnp.where(earlier, 1.0, 0.0).astype(BF16), 1, 0)
    mine = rank == (iota((slots, LANES), 0) % CAP).astype(F32)
    spread = jnp.where(mine, named, 0.0).astype(BF16)
    weighted = jnp.where(mine, weight, 0.0).astype(BF16)
    spread_ref[...] = spread
    rows = GROUP * BLOCK
    row = iota((rows, GROUP_SLOTS), 0)
    expand = (row // BLOCK) * CAP + row % CAP == iota((rows, GROUP_SLOTS), 1)
    expand = jnp.where(expand, 1.0, 0.0).astype(BF16)
    piece = (iota((rows, LANES), 0) % BLOCK) // CAP == iota((rows, LANES), 1) // tok
    for part, (chosen, ref) in enumerate(((spread, tokens_ref), (weighted, grads_ref))):
        loads[part + 1].wait()
        pieces = [ref[:, j * WIDE : (j + 1) * WIDE] for j in range(PIECES)]
        source = jnp.concatenate(pieces, axis=0)
        for g in range(slots // GROUP_SLOTS):
            picked = chosen[g * GROUP_SLOTS : (g + 1) * GROUP_SLOTS]
            select = jnp.where(piece, dot(expand, picked, 1, 0), 0.0).astype(BF16)
            block = dot(select, source, 1, 0).astype(BF16)
            out_ref[g * GROUP : (g + 1) * GROUP, part * BLOCK : (part + 1) * BLOCK, :] = (
                block.reshape(GROUP, BLOCK, WIDE)
            )


def store_part(down, gate_up, ref):
    at = 0
    for part in (gate_up, down):
        rows = part.shape[0]
        for b in range(part.shape[1] // LANES):
            ref[at : at + rows, :] = part[:, b * LANES : (b + 1) * LANES]
            at += rows


def expert_body(
    order_ref, arrived_hbm, gate_hbm, up_hbm, down_hbm,
    rows_ref, hidden_ref, slopes_ref, score_ref, far_ref,
    arrived_ref, w_gate, w_up, w_down, turned_ref, arrived_sems, load_sems,
):
    arrivals = [
        pltpu.make_async_copy(
            arrived_hbm.at[:, pl.ds(part * BLOCK, BLOCK)], arrived_ref.at[part], arrived_sems.at[part]
        )
        for part in range(2)
    ]
    loads = [
        pltpu.make_async_copy(source, target, load_sems.at[i])
        for i, (source, target) in enumerate(
            ((gate_hbm, w_gate), (up_hbm, w_up), (down_hbm, w_down))
        )
    ]
    for load in arrivals + loads:
        load.start()
    slots = rows_ref.shape[1]
    hidden = w_gate.shape[1]
    order = iota((GROUP * BLOCK, GROUP * BLOCK), 0)
    wanted = (order // CAP % GROUP) * BLOCK + (order // GROUP_SLOTS) * CAP + order % CAP
    shuffle = jnp.where(wanted == iota(order.shape, 1), 1.0, 0.0).astype(BF16)
    for part in range(2):
        arrivals[part].wait()
        for g in range(slots // GROUP_SLOTS):
            block = arrived_ref[part, g * GROUP : (g + 1) * GROUP]
            block = dot(shuffle, block.reshape(GROUP * BLOCK, WIDE), 1, 0).astype(BF16)
            for j in range(PIECES):
                rows_ref[
                    part, g * GROUP_SLOTS : (g + 1) * GROUP_SLOTS, j * WIDE : (j + 1) * WIDE
                ] = block[j * GROUP_SLOTS : (j + 1) * GROUP_SLOTS]
    loads[0].wait()
    gate_pre = dot(rows_ref[0], w_gate[...], 1, 0)
    loads[1].wait()
    up_pre = dot(rows_ref[0], w_up[...], 1, 0)
    loads[2].wait()
    grad_act = dot(rows_ref[1], w_down[...], 1, 1)
    sigmoid_gate = 1.0 / (1.0 + jnp.exp(-gate_pre))
    silu_gate = gate_pre * sigmoid_gate
    hidden_act = (silu_gate * up_pre).astype(BF16)
    slope = up_pre * sigmoid_gate * (1.0 + gate_pre * (1.0 - sigmoid_gate))
    slopes_ref[:, :hidden] = (grad_act * slope).astype(BF16)
    slopes_ref[:, hidden:] = (grad_act * silu_gate).astype(BF16)
    score = jnp.sum(hidden_act.astype(F32) * grad_act, axis=1, keepdims=True)
    score_ref[...] = jnp.broadcast_to(score, score_ref.shape).astype(BF16)

    hidden_ref[...] = hidden_act
    turned_ref[...] = hidden_act.astype(F32).T.astype(BF16)
    shards = order_ref.shape[0]
    share = hidden // shards
    target = order_ref[shards // 2]
    columns = pl.ds(pl.multiple_of(target * WIDE, WIDE), WIDE)
    gate_up = dot(rows_ref[0, :, columns], slopes_ref[...], 0, 0).astype(BF16)
    turned = turned_ref[pl.ds(pl.multiple_of(target * share, 16), share), :]
    down = dot(turned, rows_ref[1], 1, 0).astype(BF16)
    store_part(down, gate_up, far_ref)


def near_body(order_ref, rows_ref, hidden_ref, slopes_ref, *refs):
    near, down_ref = refs[:-1], refs[-1]
    shards = order_ref.shape[0]
    share = hidden_ref.shape[1] // shards
    for n in range(PIECES):
        columns = slice(n * WIDE, (n + 1) * WIDE)
        down_ref[:, columns] = dot(hidden_ref[...], rows_ref[1, :, columns], 0, 0).astype(BF16)
    for i, offset in enumerate((*range(shards // 2), *range(shards // 2 + 1, shards))):
        target = order_ref[offset]
        columns = pl.ds(pl.multiple_of(target * WIDE, WIDE), WIDE)
        gate_up = dot(rows_ref[0, :, columns], slopes_ref[...], 0, 0).astype(BF16)
        down = down_ref[pl.ds(pl.multiple_of(target * share, 16), share), :]
        store_part(down, gate_up, near[i])


def rows_body(slopes_ref, score_ref, gate_ref, up_ref, out_ref):
    hidden = gate_ref.shape[1]
    width = gate_ref.shape[0]
    for j in range(width // WIDE):
        columns = slice(j * WIDE, (j + 1) * WIDE)
        rows = dot(slopes_ref[:, :hidden], gate_ref[columns, :], 1, 1)
        rows = rows + dot(slopes_ref[:, hidden:], up_ref[columns, :], 1, 1)
        out_ref[:, columns] = rows.astype(BF16)
    out_ref[:, width:] = score_ref[...]


def combine_body(returned_ref, spread_ref, ids_ref, gates_ref, tokens_ref, out_gates_ref):
    top, tok = ids_ref.shape
    width = tokens_ref.shape[1]
    slots = spread_ref.shape[0]
    spread = spread_ref[:, :tok]
    for j in range(width // WIDE):
        columns = slice(j * WIDE, (j + 1) * WIDE)
        tokens_ref[:, columns] = dot(spread, returned_ref[:, columns], 0, 0).astype(BF16)
    score = returned_ref[:, width : width + tok].astype(F32) * spread.astype(F32)
    expert = iota((slots, tok), 0) // CAP
    gates = gates_ref[...].astype(F32)
    sums = [
        jnp.sum(jnp.where(expert == ids_ref[k : k + 1, :], score, 0.0), axis=0, keepdims=True)
        for k in range(top)
    ]
    out_gates_ref[...] = (jnp.concatenate(sums, axis=0) / gates).astype(BF16)


def unpack_body(own_ref, ahead_ref, behind_ref, gate_ref, up_ref, down_ref):
    hidden = gate_ref.shape[1]
    share = down_ref.shape[0]
    blocks = hidden // LANES

    def total(at, rows):
        at = slice(at, at + rows)
        parts = [ref[at, :].astype(F32) for ref in (own_ref, ahead_ref, behind_ref)]
        return (parts[0] + parts[1] + parts[2]).astype(BF16)

    for b in range(blocks):
        columns = slice(b * LANES, (b + 1) * LANES)
        gate_ref[:, columns] = total(b * WIDE, WIDE)
        up_ref[:, columns] = total((blocks + b) * WIDE, WIDE)
    for b in range(down_ref.shape[1] // LANES):
        at = 2 * blocks * WIDE + b * share
        down_ref[:, b * LANES : (b + 1) * LANES] = total(at, share)


def shaped(*shape, dtype=BF16):
    return jax.ShapeDtypeStruct(shape, dtype)


def cost(flops, bytes_accessed):
    return pl.CostEstimate(flops=flops, bytes_accessed=bytes_accessed, transcendentals=0)


def exchange(blocks):
    return lax.all_to_all(blocks, PLANE, split_axis=0, concat_axis=0, tiled=True)


def ring(phase):
    reps, nodes = lax.axis_size("rep"), lax.axis_size("node")
    pairs = []
    for r in range(reps):
        for n in range(nodes):
            step = 1 if n % 2 == phase else -1
            pairs.append((r * nodes + n, (r + step) % reps * nodes + n))
    return lambda message: lax.ppermute(message, ("rep", "node"), pairs)


def add(left, right):
    return (left.astype(F32) + right.astype(F32)).astype(BF16)


def shards(tokens, grads_out, expert_ids, gates, w_gate, w_up, w_down):
    experts = lax.axis_size("node") * lax.axis_size("local")
    reps = lax.axis_size("rep")
    tok, top = expert_ids.shape
    width = tokens.shape[1]
    hidden = w_gate.shape[2]
    slots = experts * CAP
    w_gate, w_up, w_down = w_gate[0], w_up[0], w_down[0]
    ids_t, gates_t = expert_ids.T, gates.T
    packed_rows = (2 * hidden * (width // reps) + (hidden // reps) * width) // LANES
    product = 2 * slots * width * hidden

    hbm = pl.BlockSpec(memory_space=pltpu.HBM)
    outgoing, spread = call(
        route_body,
        (shaped(experts, 2 * BLOCK, WIDE), shaped(slots, LANES)),
        [hbm] + whole(1) + [hbm] * 2,
        whole(2),
        scratch=(
            pltpu.VMEM((top, tok), I32),
            pltpu.VMEM((tok, width), BF16),
            pltpu.VMEM((tok, width), BF16),
            pltpu.SemaphoreType.DMA((3,)),
        ),
        cost=cost(4 * slots * LANES * width, 4 * slots * width),
        limit=VMEM_MOST,
    )(ids_t, gates_t, tokens, grads_out)
    arrived = exchange(outgoing)

    direction = 1 - 2 * (lax.axis_index("node") % 2)
    order = (lax.axis_index("rep") + direction * lax.iota(I32, reps) + reps) % reps
    smem = pl.BlockSpec(memory_space=pltpu.SMEM)
    routed, hidden_act, slopes, score, far = call(
        expert_body,
        (
            shaped(2, slots, width),
            shaped(slots, hidden),
            shaped(slots, 2 * hidden),
            shaped(slots, LANES),
            shaped(packed_rows, LANES),
        ),
        [smem] + [hbm] * 4,
        whole(5),
        scratch=(
            pltpu.VMEM((2, experts, BLOCK, WIDE), BF16),
            pltpu.VMEM((width, hidden), BF16),
            pltpu.VMEM((width, hidden), BF16),
            pltpu.VMEM((hidden, width), BF16),
            pltpu.VMEM((hidden, slots), BF16),
            pltpu.SemaphoreType.DMA((2,)),
            pltpu.SemaphoreType.DMA((3,)),
        ),
        cost=cost(4 * product, 10 << 20),
        limit=49 << 20,
    )(order, arrived, w_gate, w_up, w_down)
    forward, backward = ring(0), ring(1)
    first = forward(far)
    near = call(
        near_body,
        [shaped(packed_rows, LANES)] * (reps - 1),
        [smem] + whole(3),
        whole(reps - 1),
        scratch=(pltpu.VMEM((hidden, width), BF16),),
        cost=cost(3 * product, 8 << 20),
    )(order, routed, hidden_act, slopes)
    ahead = add(near[3], first)
    slopes, score, _ = lax.optimization_barrier((slopes, score, ahead))
    ahead, behind = forward(ahead), backward(near[-3])
    ahead, behind = forward(add(near[2], ahead)), backward(add(near[-2], behind))
    ahead, behind = forward(add(near[1], ahead)), backward(add(near[-1], behind))

    rows = call(
        rows_body,
        shaped(slots, width + LANES),
        whole(4),
        whole(1)[0],
        cost=cost(2 * product, 5 << 20),
    )(slopes, score, w_gate, w_up)
    returned = exchange(rows.reshape(experts, CAP, width + LANES)).reshape(slots, width + LANES)
    grad_tokens, grad_gates = call(
        combine_body,
        (shaped(tok, width), shaped(top, tok)),
        whole(4),
        whole(2),
        cost=cost(2 * slots * tok * width, 2 << 20),
    )(returned, spread, ids_t, gates_t)

    own, grad_tokens, grad_gates = lax.optimization_barrier((near[0], grad_tokens, grad_gates))
    grad_w_gate, grad_w_up, grad_w_down = call(
        unpack_body,
        (
            shaped(width // reps, hidden),
            shaped(width // reps, hidden),
            shaped(hidden // reps, width),
        ),
        whole(3),
        whole(3),
        cost=cost(0, 2 << 20),
    )(own, ahead, behind)
    return (
        grad_tokens,
        grad_gates.T,
        grad_w_gate[None],
        grad_w_up[None],
        grad_w_down[None],
    )


def solution(mesh):
    rows = P(("rep", "node", "local"), None)
    weights = P(PLANE, None, None)
    sharded = P(PLANE, "rep", None)
    return jax.shard_map(
        shards,
        mesh=mesh,
        in_specs=(rows, rows, rows, rows, weights, weights, weights),
        out_specs=(rows, rows, sharded, sharded, sharded),
        check_vma=False,
    )
```

```python
import jax
import jax.numpy as jnp
from jax import lax
from jax.experimental import pallas as pl
from jax.experimental.pallas import tpu as pltpu
from jax.sharding import PartitionSpec as P

PLANE = ("node", "local")
BF16, F32, I32 = jnp.bfloat16, jnp.float32, jnp.int32
VMEM_LIMIT, VMEM_MOST = 24 << 20, 62 << 20
CAP, PIECES, WIDE = 2, 8, 256
BLOCK = CAP * PIECES
GROUP = 16
GROUP_SLOTS = GROUP * CAP
LANES = 128


def iota(shape, dim):
    return lax.broadcasted_iota(I32, shape, dim)


def dot(left, right, left_dim, right_dim):
    return lax.dot_general(
        left, right, (((left_dim,), (right_dim,)), ((), ())), preferred_element_type=F32
    )


def whole(count):
    return [pl.BlockSpec(memory_space=pltpu.VMEM)] * count


def call(body, outs, in_specs, out_specs, scratch=(), cost=None, limit=VMEM_LIMIT):
    return pl.pallas_call(
        body,
        out_shape=outs,
        in_specs=in_specs,
        out_specs=out_specs,
        scratch_shapes=scratch,
        cost_estimate=cost,
        compiler_params=pltpu.CompilerParams(vmem_limit_bytes=limit),
    )


def route_body(
    ids_hbm, gates_ref, tokens_hbm, grads_hbm, out_ref, spread_ref,
    ids_ref, tokens_ref, grads_ref, sems,
):
    loads = [
        pltpu.make_async_copy(source, target, sems.at[i])
        for i, (source, target) in enumerate(
            ((ids_hbm, ids_ref), (tokens_hbm, tokens_ref), (grads_hbm, grads_ref))
        )
    ]
    for load in loads:
        load.start()
    top, tok = ids_ref.shape
    loads[0].wait()
    slots = spread_ref.shape[0]
    ids = jnp.concatenate([ids_ref[...]] * (LANES // tok), axis=1)
    weights = jnp.concatenate([gates_ref[...].astype(F32)] * (LANES // tok), axis=1)
    expert = iota((slots, LANES), 0) // CAP
    named = jnp.zeros((slots, LANES), F32)
    weight = jnp.zeros((slots, LANES), F32)
    for k in range(top):
        hit = expert == ids[k : k + 1]
        named = named + jnp.where(hit, 1.0, 0.0)
        weight = weight + jnp.where(hit, weights[k : k + 1], 0.0)
    before, after = iota((LANES, LANES), 0), iota((LANES, LANES), 1)
    earlier = (before // tok == after // tok) & (before < after)
    rank = dot(named.astype(BF16), jnp.where(earlier, 1.0, 0.0).astype(BF16), 1, 0)
    mine = rank == (iota((slots, LANES), 0) % CAP).astype(F32)
    spread = jnp.where(mine, named, 0.0).astype(BF16)
    weighted = jnp.where(mine, weight, 0.0).astype(BF16)
    spread_ref[...] = spread
    rows = GROUP * BLOCK
    row = iota((rows, GROUP_SLOTS), 0)
    expand = (row // BLOCK) * CAP + row % CAP == iota((rows, GROUP_SLOTS), 1)
    expand = jnp.where(expand, 1.0, 0.0).astype(BF16)
    piece = (iota((rows, LANES), 0) % BLOCK) // CAP == iota((rows, LANES), 1) // tok
    for part, (chosen, ref) in enumerate(((spread, tokens_ref), (weighted, grads_ref))):
        loads[part + 1].wait()
        pieces = [ref[:, j * WIDE : (j + 1) * WIDE] for j in range(PIECES)]
        source = jnp.concatenate(pieces, axis=0)
        for g in range(slots // GROUP_SLOTS):
            picked = chosen[g * GROUP_SLOTS : (g + 1) * GROUP_SLOTS]
            select = jnp.where(piece, dot(expand, picked, 1, 0), 0.0).astype(BF16)
            block = dot(select, source, 1, 0).astype(BF16)
            out_ref[g * GROUP : (g + 1) * GROUP, part * BLOCK : (part + 1) * BLOCK, :] = (
                block.reshape(GROUP, BLOCK, WIDE)
            )


def store_part(down, gate_up, ref):
    at = 0
    for part in (gate_up, down):
        rows = part.shape[0]
        for b in range(part.shape[1] // LANES):
            ref[at : at + rows, :] = part[:, b * LANES : (b + 1) * LANES]
            at += rows


def expert_body(
    order_ref, arrived_hbm, gate_hbm, up_hbm, down_hbm,
    rows_ref, hidden_ref, slopes_ref, score_ref, far_ref,
    arrived_ref, w_gate, w_up, w_down, turned_ref, arrived_sems, load_sems,
):
    arrivals = [
        pltpu.make_async_copy(
            arrived_hbm.at[:, pl.ds(part * BLOCK, BLOCK)], arrived_ref.at[part], arrived_sems.at[part]
        )
        for part in range(2)
    ]
    loads = [
        pltpu.make_async_copy(source, target, load_sems.at[i])
        for i, (source, target) in enumerate(
            ((gate_hbm, w_gate), (up_hbm, w_up), (down_hbm, w_down))
        )
    ]
    for load in arrivals + loads:
        load.start()
    slots = rows_ref.shape[1]
    hidden = w_gate.shape[1]
    order = iota((GROUP * BLOCK, GROUP * BLOCK), 0)
    wanted = (order // CAP % GROUP) * BLOCK + (order // GROUP_SLOTS) * CAP + order % CAP
    shuffle = jnp.where(wanted == iota(order.shape, 1), 1.0, 0.0).astype(BF16)
    for part in range(2):
        arrivals[part].wait()
        for g in range(slots // GROUP_SLOTS):
            block = arrived_ref[part, g * GROUP : (g + 1) * GROUP]
            block = dot(shuffle, block.reshape(GROUP * BLOCK, WIDE), 1, 0).astype(BF16)
            for j in range(PIECES):
                rows_ref[
                    part, g * GROUP_SLOTS : (g + 1) * GROUP_SLOTS, j * WIDE : (j + 1) * WIDE
                ] = block[j * GROUP_SLOTS : (j + 1) * GROUP_SLOTS]
    loads[0].wait()
    gate_pre = dot(rows_ref[0], w_gate[...], 1, 0)
    loads[1].wait()
    up_pre = dot(rows_ref[0], w_up[...], 1, 0)
    loads[2].wait()
    grad_act = dot(rows_ref[1], w_down[...], 1, 1)
    sigmoid_gate = 1.0 / (1.0 + jnp.exp(-gate_pre))
    silu_gate = gate_pre * sigmoid_gate
    hidden_act = (silu_gate * up_pre).astype(BF16)
    slope = up_pre * sigmoid_gate * (1.0 + gate_pre * (1.0 - sigmoid_gate))
    slopes_ref[:, :hidden] = (grad_act * slope).astype(BF16)
    slopes_ref[:, hidden:] = (grad_act * silu_gate).astype(BF16)
    score = jnp.sum(hidden_act.astype(F32) * grad_act, axis=1, keepdims=True)
    score_ref[...] = jnp.broadcast_to(score, score_ref.shape).astype(BF16)

    hidden_ref[...] = hidden_act
    turned_ref[...] = hidden_act.astype(F32).T.astype(BF16)
    shards = order_ref.shape[0]
    share = hidden // shards
    target = order_ref[shards // 2]
    columns = pl.ds(pl.multiple_of(target * WIDE, WIDE), WIDE)
    gate_up = dot(rows_ref[0, :, columns], slopes_ref[...], 0, 0).astype(BF16)
    turned = turned_ref[pl.ds(pl.multiple_of(target * share, 16), share), :]
    down = dot(turned, rows_ref[1], 1, 0).astype(BF16)
    store_part(down, gate_up, far_ref)


def near_body(order_ref, rows_hbm, hidden_ref, slopes_ref, *refs):
    near_hbm, (rows_ref, down_ref, packed_ref, load_sems, store_sems) = refs[:-5], refs[-5:]
    loads = [
        pltpu.make_async_copy(rows_hbm.at[part], rows_ref.at[part], load_sems.at[part])
        for part in range(2)
    ]
    loads[1].start()
    loads[0].start()
    shards = order_ref.shape[0]
    share = hidden_ref.shape[1] // shards
    loads[1].wait()
    for n in range(PIECES):
        columns = slice(n * WIDE, (n + 1) * WIDE)
        down_ref[:, columns] = dot(hidden_ref[...], rows_ref[1, :, columns], 0, 0).astype(BF16)
    loads[0].wait()
    stores = []
    far = shards // 2
    for distance in range(far - 1, -1, -1):
        for offset in sorted({-distance % shards, distance}, reverse=True):
            target = order_ref[offset]
            columns = pl.ds(pl.multiple_of(target * WIDE, WIDE), WIDE)
            gate_up = dot(rows_ref[0, :, columns], slopes_ref[...], 0, 0).astype(BF16)
            down = down_ref[pl.ds(pl.multiple_of(target * share, 16), share), :]
            i = offset - (offset > far)
            store_part(down, gate_up, packed_ref.at[i])
            store = pltpu.make_async_copy(packed_ref.at[i], near_hbm[i], store_sems.at[i])
            store.start()
            stores.append(store)
    for store in stores:
        store.wait()


def rows_body(slopes_ref, score_ref, gate_ref, up_ref, out_ref):
    hidden = gate_ref.shape[1]
    width = gate_ref.shape[0]
    for j in range(width // WIDE):
        columns = slice(j * WIDE, (j + 1) * WIDE)
        rows = dot(slopes_ref[:, :hidden], gate_ref[columns, :], 1, 1)
        rows = rows + dot(slopes_ref[:, hidden:], up_ref[columns, :], 1, 1)
        out_ref[:, columns] = rows.astype(BF16)
    out_ref[:, width:] = score_ref[...]


def combine_body(returned_ref, spread_ref, ids_ref, gates_ref, tokens_ref, out_gates_ref):
    top, tok = ids_ref.shape
    width = tokens_ref.shape[1]
    slots = spread_ref.shape[0]
    spread = spread_ref[:, :tok]
    for j in range(width // WIDE):
        columns = slice(j * WIDE, (j + 1) * WIDE)
        tokens_ref[:, columns] = dot(spread, returned_ref[:, columns], 0, 0).astype(BF16)
    score = returned_ref[:, width : width + tok].astype(F32) * spread.astype(F32)
    expert = iota((slots, tok), 0) // CAP
    gates = gates_ref[...].astype(F32)
    sums = [
        jnp.sum(jnp.where(expert == ids_ref[k : k + 1, :], score, 0.0), axis=0, keepdims=True)
        for k in range(top)
    ]
    out_gates_ref[...] = (jnp.concatenate(sums, axis=0) / gates).astype(BF16)


def unpack_body(own_ref, ahead_ref, behind_ref, gate_ref, up_ref, down_ref):
    hidden = gate_ref.shape[1]
    share = down_ref.shape[0]
    blocks = hidden // LANES

    def total(at, rows):
        at = slice(at, at + rows)
        parts = [ref[at, :].astype(F32) for ref in (own_ref, ahead_ref, behind_ref)]
        return (parts[0] + parts[1] + parts[2]).astype(BF16)

    for b in range(blocks):
        columns = slice(b * LANES, (b + 1) * LANES)
        gate_ref[:, columns] = total(b * WIDE, WIDE)
        up_ref[:, columns] = total((blocks + b) * WIDE, WIDE)
    for b in range(down_ref.shape[1] // LANES):
        at = 2 * blocks * WIDE + b * share
        down_ref[:, b * LANES : (b + 1) * LANES] = total(at, share)


def shaped(*shape, dtype=BF16):
    return jax.ShapeDtypeStruct(shape, dtype)


def cost(flops, bytes_accessed):
    return pl.CostEstimate(flops=flops, bytes_accessed=bytes_accessed, transcendentals=0)


def exchange(blocks):
    return lax.all_to_all(blocks, PLANE, split_axis=0, concat_axis=0, tiled=True)


def ring(phase):
    reps, nodes = lax.axis_size("rep"), lax.axis_size("node")
    pairs = []
    for r in range(reps):
        for n in range(nodes):
            step = 1 if n % 2 == phase else -1
            pairs.append((r * nodes + n, (r + step) % reps * nodes + n))
    return lambda message: lax.ppermute(message, ("rep", "node"), pairs)


def add(left, right):
    return (left.astype(F32) + right.astype(F32)).astype(BF16)


def shards(tokens, grads_out, expert_ids, gates, w_gate, w_up, w_down):
    experts = lax.axis_size("node") * lax.axis_size("local")
    reps = lax.axis_size("rep")
    tok, top = expert_ids.shape
    width = tokens.shape[1]
    hidden = w_gate.shape[2]
    slots = experts * CAP
    w_gate, w_up, w_down = w_gate[0], w_up[0], w_down[0]
    ids_t, gates_t = expert_ids.T, gates.T
    packed_rows = (2 * hidden * (width // reps) + (hidden // reps) * width) // LANES
    product = 2 * slots * width * hidden

    hbm = pl.BlockSpec(memory_space=pltpu.HBM)
    outgoing, spread = call(
        route_body,
        (shaped(experts, 2 * BLOCK, WIDE), shaped(slots, LANES)),
        [hbm] + whole(1) + [hbm] * 2,
        whole(2),
        scratch=(
            pltpu.VMEM((top, tok), I32),
            pltpu.VMEM((tok, width), BF16),
            pltpu.VMEM((tok, width), BF16),
            pltpu.SemaphoreType.DMA((3,)),
        ),
        cost=cost(4 * slots * LANES * width, 4 * slots * width),
        limit=VMEM_MOST,
    )(ids_t, gates_t, tokens, grads_out)
    arrived = exchange(outgoing)

    direction = 1 - 2 * (lax.axis_index("node") % 2)
    order = (lax.axis_index("rep") + direction * lax.iota(I32, reps) + reps) % reps
    smem = pl.BlockSpec(memory_space=pltpu.SMEM)
    routed, hidden_act, slopes, score, far = call(
        expert_body,
        (
            shaped(2, slots, width),
            shaped(slots, hidden),
            shaped(slots, 2 * hidden),
            shaped(slots, LANES),
            shaped(packed_rows, LANES),
        ),
        [smem] + [hbm] * 4,
        whole(5),
        scratch=(
            pltpu.VMEM((2, experts, BLOCK, WIDE), BF16),
            pltpu.VMEM((width, hidden), BF16),
            pltpu.VMEM((width, hidden), BF16),
            pltpu.VMEM((hidden, width), BF16),
            pltpu.VMEM((hidden, slots), BF16),
            pltpu.SemaphoreType.DMA((2,)),
            pltpu.SemaphoreType.DMA((3,)),
        ),
        cost=cost(4 * product, 10 << 20),
        limit=VMEM_MOST,
    )(order, arrived, w_gate, w_up, w_down)
    forward, backward = ring(0), ring(1)
    first = forward(far)
    near = call(
        near_body,
        [shaped(packed_rows, LANES)] * (reps - 1),
        [smem, hbm] + whole(2),
        [hbm] * (reps - 1),
        scratch=(
            pltpu.VMEM((2, slots, width), BF16),
            pltpu.VMEM((hidden, width), BF16),
            pltpu.VMEM((reps - 1, packed_rows, LANES), BF16),
            pltpu.SemaphoreType.DMA((2,)),
            pltpu.SemaphoreType.DMA((reps - 1,)),
        ),
        cost=cost(3 * product, 8 << 20),
        limit=VMEM_MOST,
    )(order, routed, hidden_act, slopes)
    slopes, score, _ = lax.optimization_barrier((slopes, score, near[-3]))
    ahead, behind = forward(add(near[3], first)), backward(near[-3])
    ahead, behind = forward(add(near[2], ahead)), backward(add(near[-2], behind))
    ahead, behind = forward(add(near[1], ahead)), backward(add(near[-1], behind))

    rows = call(
        rows_body,
        shaped(slots, width + LANES),
        whole(4),
        whole(1)[0],
        cost=cost(2 * product, 5 << 20),
        limit=VMEM_MOST,
    )(slopes, score, w_gate, w_up)
    returned = exchange(rows.reshape(experts, CAP, width + LANES)).reshape(slots, width + LANES)
    grad_tokens, grad_gates = call(
        combine_body,
        (shaped(tok, width), shaped(top, tok)),
        whole(4),
        whole(2),
        cost=cost(2 * slots * tok * width, 2 << 20),
    )(returned, spread, ids_t, gates_t)

    own, grad_tokens, grad_gates = lax.optimization_barrier((near[0], grad_tokens, grad_gates))
    grad_w_gate, grad_w_up, grad_w_down = call(
        unpack_body,
        (
            shaped(width // reps, hidden),
            shaped(width // reps, hidden),
            shaped(hidden // reps, width),
        ),
        whole(3),
        whole(3),
        cost=cost(0, 2 << 20),
    )(own, ahead, behind)
    return (
        grad_tokens,
        grad_gates.T,
        grad_w_gate[None],
        grad_w_up[None],
        grad_w_down[None],
    )


def solution(mesh):
    rows = P(("rep", "node", "local"), None)
    weights = P(PLANE, None, None)
    sharded = P(PLANE, "rep", None)
    return jax.shard_map(
        shards,
        mesh=mesh,
        in_specs=(rows, rows, rows, rows, weights, weights, weights),
        out_specs=(rows, rows, sharded, sharded, sharded),
        check_vma=False,
    )
```

```python
import jax
import jax.numpy as jnp
from jax import lax
from jax.experimental import pallas as pl
from jax.experimental.pallas import tpu as pltpu
from jax.sharding import PartitionSpec as P

PLANE = ("node", "local")
BF16, F32, I32 = jnp.bfloat16, jnp.float32, jnp.int32
VMEM_LEAST, VMEM_LIMIT, VMEM_MOST = 16 << 20, 50 << 20, 62 << 20
CAP, PIECES, WIDE = 2, 8, 256
BLOCK = CAP * PIECES
GROUP = 16
GROUP_SLOTS = GROUP * CAP
LANES = 128


def iota(shape, dim):
    return lax.broadcasted_iota(I32, shape, dim)


def dot(left, right, left_dim, right_dim):
    return lax.dot_general(
        left, right, (((left_dim,), (right_dim,)), ((), ())), preferred_element_type=F32
    )


def whole(count):
    return [pl.BlockSpec(memory_space=pltpu.VMEM)] * count


def call(body, outs, in_specs, out_specs, scratch=(), cost=None, limit=VMEM_LIMIT):
    return pl.pallas_call(
        body,
        out_shape=outs,
        in_specs=in_specs,
        out_specs=out_specs,
        scratch_shapes=scratch,
        cost_estimate=cost,
        compiler_params=pltpu.CompilerParams(vmem_limit_bytes=limit),
    )


def route_body(
    ids_hbm, gates_ref, tokens_hbm, grads_hbm, out_ref, spread_ref,
    ids_ref, tokens_ref, grads_ref, sems,
):
    loads = [
        pltpu.make_async_copy(source, target, sems.at[i])
        for i, (source, target) in enumerate(
            ((ids_hbm, ids_ref), (tokens_hbm, tokens_ref), (grads_hbm, grads_ref))
        )
    ]
    for load in loads:
        load.start()
    top, tok = ids_ref.shape
    loads[0].wait()
    slots = spread_ref.shape[0]
    ids = jnp.concatenate([ids_ref[...]] * (LANES // tok), axis=1)
    weights = jnp.concatenate([gates_ref[...].astype(F32)] * (LANES // tok), axis=1)
    expert = iota((slots, LANES), 0) // CAP
    named = jnp.zeros((slots, LANES), F32)
    weight = jnp.zeros((slots, LANES), F32)
    for k in range(top):
        hit = expert == ids[k : k + 1]
        named = named + jnp.where(hit, 1.0, 0.0)
        weight = weight + jnp.where(hit, weights[k : k + 1], 0.0)
    before, after = iota((LANES, LANES), 0), iota((LANES, LANES), 1)
    earlier = (before // tok == after // tok) & (before < after)
    rank = dot(named.astype(BF16), jnp.where(earlier, 1.0, 0.0).astype(BF16), 1, 0)
    mine = rank == (iota((slots, LANES), 0) % CAP).astype(F32)
    spread = jnp.where(mine, named, 0.0).astype(BF16)
    weighted = jnp.where(mine, weight, 0.0).astype(BF16)
    spread_ref[...] = spread
    rows = GROUP * BLOCK
    row = iota((rows, GROUP_SLOTS), 0)
    expand = (row // BLOCK) * CAP + row % CAP == iota((rows, GROUP_SLOTS), 1)
    expand = jnp.where(expand, 1.0, 0.0).astype(BF16)
    piece = (iota((rows, LANES), 0) % BLOCK) // CAP == iota((rows, LANES), 1) // tok
    for part, (chosen, ref) in enumerate(((spread, tokens_ref), (weighted, grads_ref))):
        loads[part + 1].wait()
        pieces = [ref[:, j * WIDE : (j + 1) * WIDE] for j in range(PIECES)]
        source = jnp.concatenate(pieces, axis=0)
        for g in range(slots // GROUP_SLOTS):
            picked = chosen[g * GROUP_SLOTS : (g + 1) * GROUP_SLOTS]
            select = jnp.where(piece, dot(expand, picked, 1, 0), 0.0).astype(BF16)
            block = dot(select, source, 1, 0).astype(BF16)
            out_ref[g * GROUP : (g + 1) * GROUP, part * BLOCK : (part + 1) * BLOCK, :] = (
                block.reshape(GROUP, BLOCK, WIDE)
            )


def store_part(down, gate_up, ref):
    at = 0
    for part in (gate_up, down):
        rows = part.shape[0]
        for b in range(part.shape[1] // LANES):
            ref[at : at + rows, :] = part[:, b * LANES : (b + 1) * LANES]
            at += rows


def expert_body(
    order_ref, arrived_ref, gate_hbm, up_hbm, down_hbm,
    slopes_ref, score_ref, *refs,
):
    parts, (rows_ref, w_gate, w_up, w_down, down_ref, load_sems) = refs[:-6], refs[-6:]
    loads = [
        pltpu.make_async_copy(source, target, load_sems.at[i])
        for i, (source, target) in enumerate(
            ((gate_hbm, w_gate), (up_hbm, w_up), (down_hbm, w_down))
        )
    ]
    for load in loads:
        load.start()
    slots = rows_ref.shape[1]
    hidden = w_gate.shape[1]
    order = iota((GROUP * BLOCK, GROUP * BLOCK), 0)
    wanted = (order // CAP % GROUP) * BLOCK + (order // GROUP_SLOTS) * CAP + order % CAP
    shuffle = jnp.where(wanted == iota(order.shape, 1), 1.0, 0.0).astype(BF16)
    for part in range(2):
        for g in range(slots // GROUP_SLOTS):
            block = arrived_ref[g * GROUP : (g + 1) * GROUP, part * BLOCK : (part + 1) * BLOCK, :]
            block = dot(shuffle, block.reshape(GROUP * BLOCK, WIDE), 1, 0).astype(BF16)
            for j in range(PIECES):
                rows_ref[
                    part, g * GROUP_SLOTS : (g + 1) * GROUP_SLOTS, j * WIDE : (j + 1) * WIDE
                ] = block[j * GROUP_SLOTS : (j + 1) * GROUP_SLOTS]
    loads[0].wait()
    gate_pre = dot(rows_ref[0], w_gate[...], 1, 0)
    loads[1].wait()
    up_pre = dot(rows_ref[0], w_up[...], 1, 0)
    loads[2].wait()
    grad_act = dot(rows_ref[1], w_down[...], 1, 1)
    sigmoid_gate = 1.0 / (1.0 + jnp.exp(-gate_pre))
    silu_gate = gate_pre * sigmoid_gate
    hidden_act = (silu_gate * up_pre).astype(BF16)
    slope = up_pre * sigmoid_gate * (1.0 + gate_pre * (1.0 - sigmoid_gate))
    slopes_ref[:, :hidden] = (grad_act * slope).astype(BF16)
    slopes_ref[:, hidden:] = (grad_act * silu_gate).astype(BF16)
    score = jnp.sum(hidden_act.astype(F32) * grad_act, axis=1, keepdims=True)
    score_ref[...] = jnp.broadcast_to(score, score_ref.shape).astype(BF16)

    shards = order_ref.shape[0]
    share = hidden // shards
    for n in range(PIECES):
        columns = slice(n * WIDE, (n + 1) * WIDE)
        down_ref[:, columns] = dot(hidden_act, rows_ref[1, :, columns], 0, 0).astype(BF16)
    for offset in range(shards):
        target = order_ref[offset]
        columns = pl.ds(pl.multiple_of(target * WIDE, WIDE), WIDE)
        gate_up = dot(rows_ref[0, :, columns], slopes_ref[...], 0, 0).astype(BF16)
        down = down_ref[pl.ds(pl.multiple_of(target * share, 16), share), :]
        store_part(down, gate_up, parts[offset])


def rows_body(slopes_ref, score_ref, gate_ref, up_ref, out_ref):
    hidden = gate_ref.shape[1]
    width = gate_ref.shape[0]
    for j in range(width // WIDE):
        columns = slice(j * WIDE, (j + 1) * WIDE)
        rows = dot(slopes_ref[:, :hidden], gate_ref[columns, :], 1, 1)
        rows = rows + dot(slopes_ref[:, hidden:], up_ref[columns, :], 1, 1)
        out_ref[:, columns] = rows.astype(BF16)
    out_ref[:, width:] = score_ref[...]


def combine_body(returned_ref, spread_ref, ids_ref, gates_ref, tokens_ref, out_gates_ref):
    top, tok = ids_ref.shape
    width = tokens_ref.shape[1]
    slots = spread_ref.shape[0]
    spread = spread_ref[:, :tok]
    for j in range(width // WIDE):
        columns = slice(j * WIDE, (j + 1) * WIDE)
        tokens_ref[:, columns] = dot(spread, returned_ref[:, columns], 0, 0).astype(BF16)
    score = returned_ref[:, width : width + tok].astype(F32) * spread.astype(F32)
    expert = iota((slots, tok), 0) // CAP
    gates = gates_ref[...].astype(F32)
    sums = [
        jnp.sum(jnp.where(expert == ids_ref[k : k + 1, :], score, 0.0), axis=0, keepdims=True)
        for k in range(top)
    ]
    out_gates_ref[...] = (jnp.concatenate(sums, axis=0) / gates).astype(BF16)


def unpack_body(own_ref, ahead_ref, behind_ref, gate_ref, up_ref, down_ref):
    hidden = gate_ref.shape[1]
    share = down_ref.shape[0]
    blocks = hidden // LANES

    def total(at, rows):
        at = slice(at, at + rows)
        parts = [ref[at, :].astype(F32) for ref in (own_ref, ahead_ref, behind_ref)]
        return (parts[0] + parts[1] + parts[2]).astype(BF16)

    for b in range(blocks):
        columns = slice(b * LANES, (b + 1) * LANES)
        gate_ref[:, columns] = total(b * WIDE, WIDE)
        up_ref[:, columns] = total((blocks + b) * WIDE, WIDE)
    for b in range(down_ref.shape[1] // LANES):
        at = 2 * blocks * WIDE + b * share
        down_ref[:, b * LANES : (b + 1) * LANES] = total(at, share)


def shaped(*shape, dtype=BF16):
    return jax.ShapeDtypeStruct(shape, dtype)


def cost(flops, bytes_accessed):
    return pl.CostEstimate(flops=flops, bytes_accessed=bytes_accessed, transcendentals=0)


def exchange(blocks):
    return lax.all_to_all(blocks, PLANE, split_axis=0, concat_axis=0, tiled=True)


def ring(phase):
    reps, nodes = lax.axis_size("rep"), lax.axis_size("node")
    pairs = []
    for r in range(reps):
        for n in range(nodes):
            step = 1 if n % 2 == phase else -1
            pairs.append((r * nodes + n, (r + step) % reps * nodes + n))
    return lambda message: lax.ppermute(message, ("rep", "node"), pairs)


def add(left, right):
    return (left.astype(F32) + right.astype(F32)).astype(BF16)


def shards(tokens, grads_out, expert_ids, gates, w_gate, w_up, w_down):
    experts = lax.axis_size("node") * lax.axis_size("local")
    reps = lax.axis_size("rep")
    tok, top = expert_ids.shape
    width = tokens.shape[1]
    hidden = w_gate.shape[2]
    slots = experts * CAP
    w_gate, w_up, w_down = w_gate[0], w_up[0], w_down[0]
    ids_t, gates_t = expert_ids.T, gates.T
    packed_rows = (2 * hidden * (width // reps) + (hidden // reps) * width) // LANES
    product = 2 * slots * width * hidden

    hbm = pl.BlockSpec(memory_space=pltpu.HBM)
    outgoing, spread = call(
        route_body,
        (shaped(experts, 2 * BLOCK, WIDE), shaped(slots, LANES)),
        [hbm] + whole(1) + [hbm] * 2,
        whole(2),
        scratch=(
            pltpu.VMEM((top, tok), I32),
            pltpu.VMEM((tok, width), BF16),
            pltpu.VMEM((tok, width), BF16),
            pltpu.SemaphoreType.DMA((3,)),
        ),
        cost=cost(4 * slots * LANES * width, 4 * slots * width),
        limit=VMEM_MOST,
    )(ids_t, gates_t, tokens, grads_out)
    arrived = exchange(outgoing)

    direction = 1 - 2 * (lax.axis_index("node") % 2)
    order = (lax.axis_index("rep") + direction * lax.iota(I32, reps) + reps) % reps
    slopes, score, *parts = call(
        expert_body,
        (
            shaped(slots, 2 * hidden),
            shaped(slots, LANES),
            *[shaped(packed_rows, LANES)] * reps,
        ),
        [pl.BlockSpec(memory_space=pltpu.SMEM)] + whole(1) + [hbm] * 3,
        whole(2 + reps),
        scratch=(
            pltpu.VMEM((2, slots, width), BF16),
            pltpu.VMEM((width, hidden), BF16),
            pltpu.VMEM((width, hidden), BF16),
            pltpu.VMEM((hidden, width), BF16),
            pltpu.VMEM((hidden, width), BF16),
            pltpu.SemaphoreType.DMA((3,)),
        ),
        cost=cost(6 * product, 12 << 20),
    )(order, arrived, w_gate, w_up, w_down)

    forward, backward = ring(0), ring(1)
    ahead, behind = forward(parts[4]), backward(parts[-3])
    ahead, behind = forward(add(parts[3], ahead)), backward(add(parts[-2], behind))
    ahead, behind = forward(add(parts[2], ahead)), backward(add(parts[-1], behind))
    ahead = forward(add(parts[1], ahead))

    rows = call(
        rows_body,
        shaped(slots, width + LANES),
        whole(4),
        whole(1)[0],
        cost=cost(2 * product, 5 << 20),
        limit=VMEM_LEAST,
    )(slopes, score, w_gate, w_up)
    returned = exchange(rows.reshape(experts, CAP, width + LANES)).reshape(slots, width + LANES)
    grad_tokens, grad_gates = call(
        combine_body,
        (shaped(tok, width), shaped(top, tok)),
        whole(4),
        whole(2),
        cost=cost(2 * slots * tok * width, 2 << 20),
        limit=VMEM_LEAST,
    )(returned, spread, ids_t, gates_t)

    own, grad_tokens, grad_gates = lax.optimization_barrier((parts[0], grad_tokens, grad_gates))
    grad_w_gate, grad_w_up, grad_w_down = call(
        unpack_body,
        (
            shaped(width // reps, hidden),
            shaped(width // reps, hidden),
            shaped(hidden // reps, width),
        ),
        whole(3),
        whole(3),
        cost=cost(0, 2 << 20),
        limit=VMEM_LEAST,
    )(own, ahead, behind)
    return (
        grad_tokens,
        grad_gates.T,
        grad_w_gate[None],
        grad_w_up[None],
        grad_w_down[None],
    )


def solution(mesh):
    rows = P(("rep", "node", "local"), None)
    weights = P(PLANE, None, None)
    sharded = P(PLANE, "rep", None)
    return jax.shard_map(
        shards,
        mesh=mesh,
        in_specs=(rows, rows, rows, rows, weights, weights, weights),
        out_specs=(rows, rows, sharded, sharded, sharded),
        check_vma=False,
    )
```

```python
import jax
import jax.numpy as jnp
from jax import lax
from jax.experimental import pallas as pl
from jax.experimental.pallas import tpu as pltpu
from jax.sharding import PartitionSpec as P

PLANE = ("node", "local")
BF16, F32, I32 = jnp.bfloat16, jnp.float32, jnp.int32
VMEM_LEAST, VMEM_LIMIT, VMEM_MOST = 16 << 20, 50 << 20, 62 << 20
CAP, PIECES, WIDE = 2, 8, 256
BLOCK = CAP * PIECES
GROUP = 16
GROUP_SLOTS = GROUP * CAP
LANES = 128
EARLY, LATE = (4, 5, 3), (6, 2, 7, 1, 0)


def iota(shape, dim):
    return lax.broadcasted_iota(I32, shape, dim)


def dot(left, right, left_dim, right_dim):
    return lax.dot_general(
        left, right, (((left_dim,), (right_dim,)), ((), ())), preferred_element_type=F32
    )


def whole(count):
    return [pl.BlockSpec(memory_space=pltpu.VMEM)] * count


def call(body, outs, in_specs, out_specs, scratch=(), cost=None, limit=VMEM_LIMIT):
    return pl.pallas_call(
        body,
        out_shape=outs,
        in_specs=in_specs,
        out_specs=out_specs,
        scratch_shapes=scratch,
        cost_estimate=cost,
        compiler_params=pltpu.CompilerParams(vmem_limit_bytes=limit),
    )


def route_body(
    ids_hbm, gates_ref, tokens_hbm, grads_hbm, out_ref, spread_ref,
    ids_ref, tokens_ref, grads_ref, sems,
):
    loads = [
        pltpu.make_async_copy(source, target, sems.at[i])
        for i, (source, target) in enumerate(
            ((ids_hbm, ids_ref), (tokens_hbm, tokens_ref), (grads_hbm, grads_ref))
        )
    ]
    for load in loads:
        load.start()
    top, tok = ids_ref.shape
    loads[0].wait()
    slots = spread_ref.shape[0]
    ids = jnp.concatenate([ids_ref[...]] * (LANES // tok), axis=1)
    weights = jnp.concatenate([gates_ref[...].astype(F32)] * (LANES // tok), axis=1)
    expert = iota((slots, LANES), 0) // CAP
    named = jnp.zeros((slots, LANES), F32)
    weight = jnp.zeros((slots, LANES), F32)
    for k in range(top):
        hit = expert == ids[k : k + 1]
        named = named + jnp.where(hit, 1.0, 0.0)
        weight = weight + jnp.where(hit, weights[k : k + 1], 0.0)
    before, after = iota((LANES, LANES), 0), iota((LANES, LANES), 1)
    earlier = (before // tok == after // tok) & (before < after)
    rank = dot(named.astype(BF16), jnp.where(earlier, 1.0, 0.0).astype(BF16), 1, 0)
    mine = rank == (iota((slots, LANES), 0) % CAP).astype(F32)
    spread = jnp.where(mine, named, 0.0).astype(BF16)
    weighted = jnp.where(mine, weight, 0.0).astype(BF16)
    spread_ref[...] = spread
    rows = GROUP * BLOCK
    row = iota((rows, GROUP_SLOTS), 0)
    expand = (row // BLOCK) * CAP + row % CAP == iota((rows, GROUP_SLOTS), 1)
    expand = jnp.where(expand, 1.0, 0.0).astype(BF16)
    piece = (iota((rows, LANES), 0) % BLOCK) // CAP == iota((rows, LANES), 1) // tok
    for part, (chosen, ref) in enumerate(((spread, tokens_ref), (weighted, grads_ref))):
        loads[part + 1].wait()
        pieces = [ref[:, j * WIDE : (j + 1) * WIDE] for j in range(PIECES)]
        source = jnp.concatenate(pieces, axis=0)
        for g in range(slots // GROUP_SLOTS):
            picked = chosen[g * GROUP_SLOTS : (g + 1) * GROUP_SLOTS]
            select = jnp.where(piece, dot(expand, picked, 1, 0), 0.0).astype(BF16)
            block = dot(select, source, 1, 0).astype(BF16)
            out_ref[g * GROUP : (g + 1) * GROUP, part * BLOCK : (part + 1) * BLOCK, :] = (
                block.reshape(GROUP, BLOCK, WIDE)
            )


def store_part(down, gate_up, ref):
    at = 0
    for part in (gate_up, down):
        rows = part.shape[0]
        for b in range(part.shape[1] // LANES):
            ref[at : at + rows, :] = part[:, b * LANES : (b + 1) * LANES]
            at += rows


def expert_body(
    order_ref, arrived_ref, gate_hbm, up_hbm, down_hbm,
    rows_ref, hidden_ref, slopes_ref, score_ref, *refs,
):
    parts, (w_gate, w_up, w_down, turned_ref, load_sems) = refs[:-5], refs[-5:]
    loads = [
        pltpu.make_async_copy(source, target, load_sems.at[i])
        for i, (source, target) in enumerate(
            ((gate_hbm, w_gate), (up_hbm, w_up), (down_hbm, w_down))
        )
    ]
    for load in loads:
        load.start()
    slots = rows_ref.shape[1]
    hidden = w_gate.shape[1]
    order = iota((GROUP * BLOCK, GROUP * BLOCK), 0)
    wanted = (order // CAP % GROUP) * BLOCK + (order // GROUP_SLOTS) * CAP + order % CAP
    shuffle = jnp.where(wanted == iota(order.shape, 1), 1.0, 0.0).astype(BF16)
    for part in range(2):
        for g in range(slots // GROUP_SLOTS):
            block = arrived_ref[g * GROUP : (g + 1) * GROUP, part * BLOCK : (part + 1) * BLOCK, :]
            block = dot(shuffle, block.reshape(GROUP * BLOCK, WIDE), 1, 0).astype(BF16)
            for j in range(PIECES):
                rows_ref[
                    part, g * GROUP_SLOTS : (g + 1) * GROUP_SLOTS, j * WIDE : (j + 1) * WIDE
                ] = block[j * GROUP_SLOTS : (j + 1) * GROUP_SLOTS]
    loads[0].wait()
    gate_pre = dot(rows_ref[0], w_gate[...], 1, 0)
    loads[1].wait()
    up_pre = dot(rows_ref[0], w_up[...], 1, 0)
    loads[2].wait()
    grad_act = dot(rows_ref[1], w_down[...], 1, 1)
    sigmoid_gate = 1.0 / (1.0 + jnp.exp(-gate_pre))
    silu_gate = gate_pre * sigmoid_gate
    hidden_act = (silu_gate * up_pre).astype(BF16)
    slope = up_pre * sigmoid_gate * (1.0 + gate_pre * (1.0 - sigmoid_gate))
    slopes_ref[:, :hidden] = (grad_act * slope).astype(BF16)
    slopes_ref[:, hidden:] = (grad_act * silu_gate).astype(BF16)
    score = jnp.sum(hidden_act.astype(F32) * grad_act, axis=1, keepdims=True)
    score_ref[...] = jnp.broadcast_to(score, score_ref.shape).astype(BF16)

    hidden_ref[...] = hidden_act
    turned_ref[...] = hidden_act.astype(F32).T.astype(BF16)
    share = hidden // order_ref.shape[0]
    for offset, part in zip(EARLY, parts, strict=True):
        target = order_ref[offset]
        columns = pl.ds(pl.multiple_of(target * WIDE, WIDE), WIDE)
        gate_up = dot(rows_ref[0, :, columns], slopes_ref[...], 0, 0).astype(BF16)
        turned = turned_ref[pl.ds(pl.multiple_of(target * share, 16), share), :]
        store_part(dot(turned, rows_ref[1], 1, 0).astype(BF16), gate_up, part)


def late_body(order_ref, rows_ref, hidden_ref, slopes_ref, *refs):
    parts, down_ref = refs[:-1], refs[-1]
    share = hidden_ref.shape[1] // order_ref.shape[0]
    for n in range(PIECES):
        columns = slice(n * WIDE, (n + 1) * WIDE)
        down_ref[:, columns] = dot(hidden_ref[...], rows_ref[1, :, columns], 0, 0).astype(BF16)
    for offset, part in zip(LATE, parts, strict=True):
        target = order_ref[offset]
        columns = pl.ds(pl.multiple_of(target * WIDE, WIDE), WIDE)
        gate_up = dot(rows_ref[0, :, columns], slopes_ref[...], 0, 0).astype(BF16)
        down = down_ref[pl.ds(pl.multiple_of(target * share, 16), share), :]
        store_part(down, gate_up, part)


def rows_body(slopes_ref, score_ref, gate_ref, up_ref, out_ref):
    hidden = gate_ref.shape[1]
    width = gate_ref.shape[0]
    for j in range(width // WIDE):
        columns = slice(j * WIDE, (j + 1) * WIDE)
        rows = dot(slopes_ref[:, :hidden], gate_ref[columns, :], 1, 1)
        rows = rows + dot(slopes_ref[:, hidden:], up_ref[columns, :], 1, 1)
        out_ref[:, columns] = rows.astype(BF16)
    out_ref[:, width:] = score_ref[...]


def combine_body(returned_ref, spread_ref, ids_ref, gates_ref, tokens_ref, out_gates_ref):
    top, tok = ids_ref.shape
    width = tokens_ref.shape[1]
    slots = spread_ref.shape[0]
    spread = spread_ref[:, :tok]
    for j in range(width // WIDE):
        columns = slice(j * WIDE, (j + 1) * WIDE)
        tokens_ref[:, columns] = dot(spread, returned_ref[:, columns], 0, 0).astype(BF16)
    score = returned_ref[:, width : width + tok].astype(F32) * spread.astype(F32)
    expert = iota((slots, tok), 0) // CAP
    gates = gates_ref[...].astype(F32)
    sums = [
        jnp.sum(jnp.where(expert == ids_ref[k : k + 1, :], score, 0.0), axis=0, keepdims=True)
        for k in range(top)
    ]
    out_gates_ref[...] = (jnp.concatenate(sums, axis=0) / gates).astype(BF16)


def unpack_body(own_ref, ahead_ref, behind_ref, gate_ref, up_ref, down_ref):
    hidden = gate_ref.shape[1]
    share = down_ref.shape[0]
    blocks = hidden // LANES

    def total(at, rows):
        at = slice(at, at + rows)
        parts = [ref[at, :].astype(F32) for ref in (own_ref, ahead_ref, behind_ref)]
        return (parts[0] + parts[1] + parts[2]).astype(BF16)

    for b in range(blocks):
        columns = slice(b * LANES, (b + 1) * LANES)
        gate_ref[:, columns] = total(b * WIDE, WIDE)
        up_ref[:, columns] = total((blocks + b) * WIDE, WIDE)
    for b in range(down_ref.shape[1] // LANES):
        at = 2 * blocks * WIDE + b * share
        down_ref[:, b * LANES : (b + 1) * LANES] = total(at, share)


def shaped(*shape, dtype=BF16):
    return jax.ShapeDtypeStruct(shape, dtype)


def cost(flops, bytes_accessed):
    return pl.CostEstimate(flops=flops, bytes_accessed=bytes_accessed, transcendentals=0)


def exchange(blocks):
    return lax.all_to_all(blocks, PLANE, split_axis=0, concat_axis=0, tiled=True)


def ring(phase):
    reps, nodes = lax.axis_size("rep"), lax.axis_size("node")
    pairs = []
    for r in range(reps):
        for n in range(nodes):
            step = 1 if n % 2 == phase else -1
            pairs.append((r * nodes + n, (r + step) % reps * nodes + n))
    return lambda message: lax.ppermute(message, ("rep", "node"), pairs)


def add(left, right):
    return (left.astype(F32) + right.astype(F32)).astype(BF16)


def shards(tokens, grads_out, expert_ids, gates, w_gate, w_up, w_down):
    experts = lax.axis_size("node") * lax.axis_size("local")
    reps = lax.axis_size("rep")
    tok, top = expert_ids.shape
    width = tokens.shape[1]
    hidden = w_gate.shape[2]
    slots = experts * CAP
    w_gate, w_up, w_down = w_gate[0], w_up[0], w_down[0]
    ids_t, gates_t = expert_ids.T, gates.T
    packed_rows = (2 * hidden * (width // reps) + (hidden // reps) * width) // LANES
    product = 2 * slots * width * hidden

    hbm = pl.BlockSpec(memory_space=pltpu.HBM)
    outgoing, spread = call(
        route_body,
        (shaped(experts, 2 * BLOCK, WIDE), shaped(slots, LANES)),
        [hbm] + whole(1) + [hbm] * 2,
        whole(2),
        scratch=(
            pltpu.VMEM((top, tok), I32),
            pltpu.VMEM((tok, width), BF16),
            pltpu.VMEM((tok, width), BF16),
            pltpu.SemaphoreType.DMA((3,)),
        ),
        cost=cost(4 * slots * LANES * width, 4 * slots * width),
        limit=VMEM_MOST,
    )(ids_t, gates_t, tokens, grads_out)
    arrived = exchange(outgoing)

    direction = 1 - 2 * (lax.axis_index("node") % 2)
    order = (lax.axis_index("rep") + direction * lax.iota(I32, reps) + reps) % reps
    smem = pl.BlockSpec(memory_space=pltpu.SMEM)
    routed, hidden_act, slopes, score, *early = call(
        expert_body,
        (
            shaped(2, slots, width),
            shaped(slots, hidden),
            shaped(slots, 2 * hidden),
            shaped(slots, LANES),
            *[shaped(packed_rows, LANES)] * len(EARLY),
        ),
        [smem] + whole(1) + [hbm] * 3,
        whole(4 + len(EARLY)),
        scratch=(
            pltpu.VMEM((width, hidden), BF16),
            pltpu.VMEM((width, hidden), BF16),
            pltpu.VMEM((hidden, width), BF16),
            pltpu.VMEM((hidden, slots), BF16),
            pltpu.SemaphoreType.DMA((3,)),
        ),
        cost=cost(4 * product, 12 << 20),
    )(order, arrived, w_gate, w_up, w_down)
    parts = dict(zip(EARLY, early, strict=True))
    forward, backward = ring(0), ring(1)
    ahead, behind = forward(parts[4]), backward(parts[5])
    to_ahead = add(parts[3], ahead)
    later, _ = lax.optimization_barrier((slopes, to_ahead))
    late = call(
        late_body,
        [shaped(packed_rows, LANES)] * len(LATE),
        [smem] + whole(3),
        whole(len(LATE)),
        scratch=(pltpu.VMEM((hidden, width), BF16),),
        cost=cost(3 * product, 8 << 20),
        limit=VMEM_LEAST,
    )(order, routed, hidden_act, later)
    parts |= dict(zip(LATE, late, strict=True))
    ahead, behind = forward(to_ahead), backward(add(parts[6], behind))
    ahead, behind = forward(add(parts[2], ahead)), backward(add(parts[7], behind))
    ahead = forward(add(parts[1], ahead))

    rows = call(
        rows_body,
        shaped(slots, width + LANES),
        whole(4),
        whole(1)[0],
        cost=cost(2 * product, 5 << 20),
        limit=VMEM_LEAST,
    )(slopes, score, w_gate, w_up)
    returned = exchange(rows.reshape(experts, CAP, width + LANES)).reshape(slots, width + LANES)
    grad_tokens, grad_gates = call(
        combine_body,
        (shaped(tok, width), shaped(top, tok)),
        whole(4),
        whole(2),
        cost=cost(2 * slots * tok * width, 2 << 20),
        limit=VMEM_LEAST,
    )(returned, spread, ids_t, gates_t)

    own, grad_tokens, grad_gates = lax.optimization_barrier((parts[0], grad_tokens, grad_gates))
    grad_w_gate, grad_w_up, grad_w_down = call(
        unpack_body,
        (
            shaped(width // reps, hidden),
            shaped(width // reps, hidden),
            shaped(hidden // reps, width),
        ),
        whole(3),
        whole(3),
        cost=cost(0, 2 << 20),
        limit=VMEM_LEAST,
    )(own, ahead, behind)
    return (
        grad_tokens,
        grad_gates.T,
        grad_w_gate[None],
        grad_w_up[None],
        grad_w_down[None],
    )


def solution(mesh):
    rows = P(("rep", "node", "local"), None)
    weights = P(PLANE, None, None)
    sharded = P(PLANE, "rep", None)
    return jax.shard_map(
        shards,
        mesh=mesh,
        in_specs=(rows, rows, rows, rows, weights, weights, weights),
        out_specs=(rows, rows, sharded, sharded, sharded),
        check_vma=False,
    )
```
